128 devices in a mesh: grp: 8 (over x, core), tp: 16 (over z, y).
Axes of the slice: x: 4, y: 4, z: 4, core: 2. Of those that a mesh axis runs over, the one named last changes fastest.
Arguments:
- activations: bfloat16 [4096, 8192], P('grp', 'tp'), may hold values from -6 to 6
- output_gradient: bfloat16 [4096, 8192], P('grp', 'tp'), may hold values from -6 to 6
- frozen_weight: bfloat16 [8192, 8192], P(None, 'tp'), may hold values from -0.0625 to 0.0625
- adapter_down_factors: bfloat16 [128, 32, 8192], P('grp', None, 'tp'), may hold values from -6 to 6
- adapter_up_factors: bfloat16 [128, 32, 8192], P('grp', None, 'tp'), may hold values from -6 to 6
- first_moment_down: float32 [128, 32, 8192], P('grp', None, 'tp'), may hold values from -6 to 6
- second_moment_down: float32 [128, 32, 8192], P('grp', None, 'tp'), may hold values from 0.5 to 2
- first_moment_up: float32 [128, 32, 8192], P('grp', None, 'tp'), may hold values from -6 to 6
- second_moment_up: float32 [128, 32, 8192], P('grp', None, 'tp'), may hold values from 0.5 to 2
- sample_row_prompt: int32 [8, 512], P('grp'), may hold values from 0 to 15, never falling along the last dimension, each value on 1 to 128 neighbouring positions
- majority_vote_reward: int32 [8, 512], P('grp'), may hold values 0 or 1
- prompt_adapter_slot: int32 [128], replicated, may hold values from 0 to 127, as said below
Outputs:
- layer_out: bfloat16 [4096, 8192], P('grp', 'tp')
- input_grad: bfloat16 [4096, 8192], P('grp', 'tp')
- updated_down_factors: bfloat16 [128, 32, 8192], P('grp', None, 'tp')
- updated_up_factors: bfloat16 [128, 32, 8192], P('grp', None, 'tp')
- updated_first_down: float32 [128, 32, 8192], P('grp', None, 'tp')
- updated_second_down: float32 [128, 32, 8192], P('grp', None, 'tp')
- updated_first_up: float32 [128, 32, 8192], P('grp', None, 'tp')
- updated_second_up: float32 [128, 32, 8192], P('grp', None, 'tp')
The draws below stay inside these ranges and needn't reach their ends.
Inputs may be any that keep to these rules, and one draw needn't show every extreme that they name: `prompt_adapter_slot`: A permutation. Slots g * 16 to (g + 1) * 16 - 1 lie in group g's shard, and each group's shard holds the slots of exactly 2 prompts of every group.
All inputs are finite; a program needn't handle non-finite values. No bound on the sum of `majority_vote_reward` on one device may be relied on, other than what follows from the above.
Results may differ from the reference program's by a relative error of at most 0.0056.
Values may be sent and summed in bfloat16 or wider, within the bound.
No kernel may reach another device: no remote copies, remote signals or barrier semaphores. Data moves between devices by JAX's collectives and lax.ppermute only.
A program may use at most 192 MiB of HBM per device.

```python
import math
import jax
import jax.numpy as jnp
import numpy as np
from jax import lax

MODEL_WIDTH = 8192
ADAPTER_RANK = 32
SHARE = 2
ROWS_GRP = 512
GROUP_PROMPTS = 16
TOTAL_PROMPTS = 128
ROWS = 4096
N_GRP = 8


def draw_prompt_adapter_slot(key, part):
    key = jax.random.fold_in(key, 11)
    first_key, second_key, third_key = jax.random.split(key, 3)
    index = jnp.arange(TOTAL_PROMPTS, dtype=jnp.int32)
    owner_score = index // GROUP_PROMPTS * TOTAL_PROMPTS + jax.random.permutation(first_key, TOTAL_PROMPTS).astype(jnp.int32)
    owner_order = jnp.argsort(owner_score).astype(jnp.int32)
    source = jnp.zeros((TOTAL_PROMPTS,), jnp.int32).at[owner_order].set(index % GROUP_PROMPTS // SHARE)
    source_score = source * TOTAL_PROMPTS + jax.random.permutation(second_key, TOTAL_PROMPTS).astype(jnp.int32)
    by_source = jnp.argsort(source_score).astype(jnp.int32)
    prompt_score = index // GROUP_PROMPTS * TOTAL_PROMPTS + jax.random.permutation(third_key, TOTAL_PROMPTS).astype(jnp.int32)
    prompt_list = jnp.argsort(prompt_score).astype(jnp.int32)
    return jnp.zeros((TOTAL_PROMPTS,), jnp.int32).at[prompt_list].set(by_source)


def touch_ends(entries, key, least, largest):
    spot = [jax.random.randint(jax.random.fold_in(key, axis), (), 0, length) for axis, length in enumerate(entries.shape)]
    widest = entries.shape.index(max(entries.shape))
    beside = spot[:widest] + [(spot[widest] + 1) % entries.shape[widest]] + spot[widest + 1:]
    return entries.at[tuple(spot)].set(least).at[tuple(beside)].set(largest)


def block_scale(rng, shape, shards, low, high):
    def one(dim, blocks):
        heights = jax.random.uniform(jax.random.fold_in(jax.random.fold_in(rng, 6), dim), (blocks,), jnp.float32, low / len(shards), high / len(shards))
        return jnp.repeat(jnp.exp(heights), shape[dim] // blocks).reshape((-1,) + (1,) * (len(shape) - dim - 1))

    gain = one(*shards[0])
    for cut in shards[1:]:
        gain = gain * one(*cut)
    return gain


def split_up(number_of, total, bound, slope):
    loads = [(1 << 20) // math.isqrt(grade ** slope) + 1 for grade in range(2, number_of + 1)]
    spare, holding = total - bound - (number_of - 1), [1] * (number_of - 1)
    while spare > 0:
        candidates = [i for i in range(number_of - 1) if holding[i] < bound]
        pool, remaining = sum([loads[i] for i in candidates]), spare
        for i in candidates:
            addition = min(bound - holding[i], max(1, remaining * loads[i] // pool), spare)
            holding[i] = holding[i] + addition
            spare = spare - addition
    return np.array([bound] + holding)


def ragged(rng, number_of, total, most, skew):
    if number_of == 2:
        one = jax.random.randint(rng, (), max(1, total - most), min(most, total - 1) + 1)
        return jnp.stack([one, total - one])
    lengths = jnp.asarray(split_up(number_of, total, most, skew), jnp.int32)
    couples = (number_of - 1) // 2
    giver, taker = lengths[1:1 + 2 * couples:2], lengths[2:2 + 2 * couples:2]
    slack = jnp.minimum(giver - 1, most - taker)
    passed = jax.random.randint(jax.random.fold_in(rng, 1), (couples,), 0, 1 << 20) % (slack + 1)
    lengths = lengths.at[1:1 + 2 * couples:2].set(giver - passed).at[2:2 + 2 * couples:2].set(taker + passed)
    return lengths[jax.random.permutation(jax.random.fold_in(rng, 2), number_of)]


def noise(key, shape, spread, limit, cuts=(), held_as=jnp.bfloat16):
    loudness = block_scale(key, shape, cuts, -0.22, 0.18) if cuts else 1.0
    drawn = jax.random.normal(key, shape, jnp.float32) * spread * loudness
    return jnp.minimum(jnp.maximum(drawn, -limit), limit).astype(held_as)


def setup_inputs(seed: int = 0) -> dict:
    seeds = jax.random.split(jax.random.key(seed), 13)
    return {
        "activations": noise(seeds[0], (ROWS, MODEL_WIDTH), 1.0, 6.0, ((0, 8), (1, 16))),
        "output_gradient": noise(seeds[1], (ROWS, MODEL_WIDTH), 1.0, 6.0, ((0, 8), (1, 16))),
        "frozen_weight": noise(seeds[2], (MODEL_WIDTH, MODEL_WIDTH), MODEL_WIDTH ** -0.5, 0.0625, ((1, 16),)),
        "adapter_down_factors": noise(seeds[3], (TOTAL_PROMPTS, ADAPTER_RANK, MODEL_WIDTH), 1.0, 6.0, ((0, 8), (2, 16))),
        "adapter_up_factors": noise(seeds[4], (TOTAL_PROMPTS, ADAPTER_RANK, MODEL_WIDTH), 1.0, 6.0, ((0, 8), (2, 16))),
        "first_moment_down": noise(seeds[5], (TOTAL_PROMPTS, ADAPTER_RANK, MODEL_WIDTH), 1.0, 6.0, ((0, 8), (2, 16)), jnp.float32),
        "second_moment_down": jnp.clip(jnp.exp(math.log(2.0) - 1.3862944 * jax.random.uniform(seeds[6], (TOTAL_PROMPTS, ADAPTER_RANK, MODEL_WIDTH), jnp.float32) ** block_scale(seeds[6], (TOTAL_PROMPTS, ADAPTER_RANK, MODEL_WIDTH), ((0, 8), (2, 16)), -0.2, 0.2)), 0.5, 2.0),
        "first_moment_up": noise(seeds[7], (TOTAL_PROMPTS, ADAPTER_RANK, MODEL_WIDTH), 1.0, 6.0, ((0, 8), (2, 16)), jnp.float32),
        "second_moment_up": jnp.clip(jnp.exp(math.log(2.0) - 1.3862944 * jax.random.uniform(seeds[8], (TOTAL_PROMPTS, ADAPTER_RANK, MODEL_WIDTH), jnp.float32) ** block_scale(seeds[8], (TOTAL_PROMPTS, ADAPTER_RANK, MODEL_WIDTH), ((0, 8), (2, 16)), -0.2, 0.2)), 0.5, 2.0),
        "sample_row_prompt": jax.vmap(lambda own: jnp.searchsorted(jnp.cumsum(ragged(own, GROUP_PROMPTS, ROWS_GRP, 4 * ROWS_GRP // GROUP_PROMPTS, 2)), jnp.arange(ROWS_GRP), side="right"))(jax.random.split(seeds[9], N_GRP)).reshape((N_GRP, ROWS_GRP)).astype(jnp.int32),
        "majority_vote_reward": touch_ends((jax.random.randint(seeds[10], (N_GRP, ROWS_GRP), 0, 2) < 1).astype(jnp.int32), jax.random.fold_in(seeds[10], 1), 0, 1),
        "prompt_adapter_slot": draw_prompt_adapter_slot(jax.random.fold_in(seeds[12], 71), 0),
    }


beta_first = 0.9
beta_second = 0.999
step_rate = 0.2
adam_eps = 1e-08
adapter_scale = 2.0

def moment_step_update(param, moment, second, grad):
    grad_full = grad.astype(jnp.float32)
    moment_new = beta_first * moment + (1.0 - beta_first) * grad_full
    second_new = beta_second * second + (1.0 - beta_second) * grad_full * grad_full
    param_new = param.astype(jnp.float32) - step_rate * moment_new / (jnp.sqrt(second_new) + adam_eps)
    return (param_new.astype(jnp.bfloat16), moment_new, second_new)

def reference(activations, output_gradient, frozen_weight, adapter_down_factors, adapter_up_factors, first_moment_down, second_moment_down, first_moment_up, second_moment_up, sample_row_prompt, majority_vote_reward, prompt_adapter_slot):
    scale_down = MODEL_WIDTH ** (-0.5)
    scaled_up_factors = adapter_scale / ADAPTER_RANK ** 0.5
    contract_cols = (((1,), (1,)), ((), ()))
    contract_rows = (((0,), (0,)), ((), ()))
    layer_parts = []
    input_parts = []
    down_grads = []
    up_grads = []
    for member in range(N_GRP):
        first = member * ROWS_GRP
        inputs = activations[first:first + ROWS_GRP]
        cotangent = output_gradient[first:first + ROWS_GRP]
        labels = sample_row_prompt[member]
        onehot = (labels[:, None] == jnp.arange(GROUP_PROMPTS, dtype=jnp.int32)[None, :]).astype(jnp.float32)
        reward = majority_vote_reward[member].astype(jnp.float32)
        counts = lax.optimization_barrier(jnp.sum(onehot, axis=0))
        mean_reward = lax.optimization_barrier(jnp.sum(onehot * reward[:, None], axis=0)) / counts
        advantage = reward - lax.optimization_barrier(jnp.sum(onehot * mean_reward[None, :], axis=1))
        weighted = (advantage[:, None] * cotangent.astype(jnp.float32)).astype(jnp.bfloat16)
        adapter_slots = prompt_adapter_slot[member * GROUP_PROMPTS:(member + 1) * GROUP_PROMPTS]
        flattened_down = jnp.take(adapter_down_factors, adapter_slots, axis=0).reshape(GROUP_PROMPTS * ADAPTER_RANK, MODEL_WIDTH)
        flattened_up = jnp.take(adapter_up_factors, adapter_slots, axis=0).reshape(GROUP_PROMPTS * ADAPTER_RANK, MODEL_WIDTH)
        low_all = lax.dot_general(inputs, flattened_down, contract_cols, preferred_element_type=jnp.float32)
        low = lax.optimization_barrier(jnp.sum(low_all.reshape(ROWS_GRP, GROUP_PROMPTS, ADAPTER_RANK) * onehot[:, :, None], axis=1))
        low = (scale_down * low).astype(jnp.bfloat16)
        back_all = lax.dot_general(weighted, flattened_up, contract_cols, preferred_element_type=jnp.float32)
        back_low = lax.optimization_barrier(jnp.sum(back_all.reshape(ROWS_GRP, GROUP_PROMPTS, ADAPTER_RANK) * onehot[:, :, None], axis=1))
        back_low = (scaled_up_factors * back_low).astype(jnp.bfloat16)
        onehot_half = onehot.astype(jnp.bfloat16)
        low_wide = (onehot_half[:, :, None] * low[:, None, :]).reshape(ROWS_GRP, GROUP_PROMPTS * ADAPTER_RANK)
        back_wide = (onehot_half[:, :, None] * back_low[:, None, :]).reshape(ROWS_GRP, GROUP_PROMPTS * ADAPTER_RANK)
        base_out = jnp.dot(inputs, frozen_weight, preferred_element_type=jnp.float32)
        layer = base_out + scaled_up_factors * jnp.dot(low_wide, flattened_up, preferred_element_type=jnp.float32)
        layer_parts.append(layer.astype(jnp.bfloat16))
        inward = lax.dot_general(weighted, frozen_weight, contract_cols, preferred_element_type=jnp.float32)
        inward = inward + scale_down * jnp.dot(back_wide, flattened_down, preferred_element_type=jnp.float32)
        input_parts.append(inward.astype(jnp.bfloat16))
        grad_down = scale_down * lax.dot_general(back_wide, inputs, contract_rows, preferred_element_type=jnp.float32)
        grad_up = scaled_up_factors * lax.dot_general(low_wide, weighted, contract_rows, preferred_element_type=jnp.float32)
        down_grads.append(grad_down.astype(jnp.bfloat16).reshape(GROUP_PROMPTS, ADAPTER_RANK, MODEL_WIDTH))
        up_grads.append(grad_up.astype(jnp.bfloat16).reshape(GROUP_PROMPTS, ADAPTER_RANK, MODEL_WIDTH))
    layer_out = jnp.concatenate(layer_parts, axis=0)
    input_grad = jnp.concatenate(input_parts, axis=0)
    by_prompt_down = jnp.concatenate(down_grads, axis=0)
    by_prompt_up = jnp.concatenate(up_grads, axis=0)
    down_factor_slot = jnp.zeros((TOTAL_PROMPTS, ADAPTER_RANK, MODEL_WIDTH), jnp.bfloat16).at[prompt_adapter_slot].set(by_prompt_down)
    up_factor_slot = jnp.zeros((TOTAL_PROMPTS, ADAPTER_RANK, MODEL_WIDTH), jnp.bfloat16).at[prompt_adapter_slot].set(by_prompt_up)
    updated_down_factors, updated_first_down, updated_second_down = moment_step_update(adapter_down_factors, first_moment_down, second_moment_down, down_factor_slot)
    updated_up_factors, updated_first_up, updated_second_up = moment_step_update(adapter_up_factors, first_moment_up, second_moment_up, up_factor_slot)
    return (layer_out, input_grad, updated_down_factors, updated_up_factors, updated_first_down, updated_second_down, updated_first_up, updated_second_up)
```

```python
import functools

import jax
import jax.numpy as jnp
from jax import lax
from jax.experimental import pallas as pl
from jax.experimental.pallas import tpu as pltpu
from jax.sharding import Mesh, PartitionSpec as P

beta_first = 0.9
beta_second = 0.999
step_rate = 0.2
adam_eps = 1e-08
adapter_scale = 2.0

WIDTH = 8192
RANK = 32
COLS = 512
HALF = 256
ROWS = 512
PROMPTS = 16
ANY = pl.BlockSpec(memory_space=pl.ANY)
VMEM = pl.BlockSpec(memory_space=pltpu.VMEM)
F32 = jnp.float32
BF16 = jnp.bfloat16


def params(mib=32):
    return pltpu.CompilerParams(vmem_limit_bytes=mib * 1024 * 1024)


def pick_kernel(slots, member, down, up, out, sem):
    g = member[0]
    for d in range(8):
        def step(p, j):
            s = slots[d * PROMPTS + p]
            mine = lax.div(s, PROMPTS) == g

            @pl.when(mine)
            def _():
                i = lax.rem(s, PROMPTS)
                pltpu.make_async_copy(down.at[i], out.at[d, j, 0], sem.at[0]).start()
                pltpu.make_async_copy(up.at[i], out.at[d, j, 1], sem.at[0]).start()

            return j + mine.astype(jnp.int32)

        lax.fori_loop(0, PROMPTS, step, jnp.int32(0))
    pltpu.make_async_copy(out, out, sem.at[0]).wait()


def pick(slots, member, down, up):
    return pl.pallas_call(
        pick_kernel,
        out_shape=jax.ShapeDtypeStruct((8, 2, 2, RANK, COLS), BF16),
        grid_spec=pltpu.PrefetchScalarGridSpec(
            num_scalar_prefetch=2,
            grid=(),
            in_specs=[ANY, ANY],
            out_specs=ANY,
            scratch_shapes=[pltpu.SemaphoreType.DMA((1,))],
        ),
        compiler_params=params(),
        cost_estimate=pl.CostEstimate(flops=0, bytes_accessed=4 << 20, transcendentals=0),
    )(slots, member, down, up)


def adam_kernel(pos, grads, dn, up, m1d, m2d, m1u, m2u, odn, oup, o1d, o2d, o1u, o2u):
    i0 = pl.program_id(0) * 4
    for k in range(4):
        q = pos[i0 + k]
        for which, (f, m1, m2, of, o1, o2) in enumerate(
            ((dn, m1d, m2d, odn, o1d, o2d), (up, m1u, m2u, oup, o1u, o2u))
        ):
            grad = grads[q, which].astype(F32)
            first = beta_first * m1[k] + (1.0 - beta_first) * grad
            second = beta_second * m2[k] + (1.0 - beta_second) * grad * grad
            of[k] = (
                f[k].astype(F32) - step_rate * first / (jnp.sqrt(second) + adam_eps)
            ).astype(BF16)
            o1[k] = first
            o2[k] = second


def adam(pos, grads, dn, up, m1d, m2d, m1u, m2u):
    block = pl.BlockSpec((4, RANK, COLS), lambda i, pos: (i, 0, 0))
    half = jax.ShapeDtypeStruct((PROMPTS, RANK, COLS), BF16)
    full = jax.ShapeDtypeStruct((PROMPTS, RANK, COLS), F32)
    return pl.pallas_call(
        adam_kernel,
        out_shape=(half, half, full, full, full, full),
        grid_spec=pltpu.PrefetchScalarGridSpec(
            num_scalar_prefetch=1,
            grid=(4,),
            in_specs=[pl.BlockSpec((PROMPTS, 2, RANK, COLS), lambda i, pos: (0, 0, 0, 0))]
            + [block] * 6,
            out_specs=[block] * 6,
        ),
        compiler_params=params(),
        cost_estimate=pl.CostEstimate(flops=8 << 20, bytes_accessed=12 << 20, transcendentals=0),
    )(pos, grads, dn, up, m1d, m2d, m1u, m2u)


def forward_kernel(where, a0, a1, a2, a3, *rest):
    pieces, out = rest[:-1], rest[-1]
    c = where[0]
    here = pl.ds(pl.multiple_of(c * HALF, HALF), HALF)
    there = pl.ds(pl.multiple_of((1 - c) * HALF, HALF), HALF)
    total = None
    for e, a in enumerate((a0, a1, a2, a3)):
        term = jnp.dot(a[:, here], pieces[e][0], preferred_element_type=F32)
        term += jnp.dot(a[:, there], pieces[4 + e][0], preferred_element_type=F32)
        total = term if total is None else total + term
    out[...] = total.astype(out.dtype)


def forward(where, blocks, own, other, d):
    piece = pl.BlockSpec((1, HALF, HALF), lambda n, w: (d - 1, 0, n))
    return pl.pallas_call(
        forward_kernel,
        out_shape=jax.ShapeDtypeStruct((ROWS, COLS), BF16),
        grid_spec=pltpu.PrefetchScalarGridSpec(
            num_scalar_prefetch=1,
            grid=(2,),
            in_specs=[pl.BlockSpec((ROWS, COLS), lambda n, w: (0, 0))] * 4 + [piece] * 8,
            out_specs=pl.BlockSpec((ROWS, HALF), lambda n, w: (0, n)),
        ),
        compiler_params=params(),
        cost_estimate=pl.CostEstimate(
            flops=2 * 512 * 512 * 2048, bytes_accessed=5 << 20, transcendentals=0
        ),
    )(where, *blocks, *own, *other)


def local_kernel(where, a0, a1, a2, a3, w0, w1, w2, w3, out):
    total = None
    for a, w in ((a0, w0), (a1, w1), (a2, w2), (a3, w3)):
        term = jnp.dot(a[...], w[...], preferred_element_type=F32)
        total = term if total is None else total + term
    out[...] = total


def forward_local(where, blocks, weight):
    def piece(e):
        return pl.BlockSpec((COLS, HALF), lambda n, w: (w[1 + e], n))

    return pl.pallas_call(
        local_kernel,
        out_shape=jax.ShapeDtypeStruct((ROWS, COLS), F32),
        grid_spec=pltpu.PrefetchScalarGridSpec(
            num_scalar_prefetch=1,
            grid=(2,),
            in_specs=[pl.BlockSpec((ROWS, COLS), lambda n, w: (0, 0))] * 4
            + [piece(e) for e in range(4)],
            out_specs=pl.BlockSpec((ROWS, HALF), lambda n, w: (0, n)),
        ),
        compiler_params=params(),
        cost_estimate=pl.CostEstimate(
            flops=2 * 512 * 512 * 2048, bytes_accessed=5 << 20, transcendentals=0
        ),
    )(where, *blocks, weight, weight, weight, weight)


def backward_kernel(where, g0, g1, g2, g3, own, other, local, out):
    c = where[0]
    here = pl.ds(pl.multiple_of(c * HALF, HALF), HALF)
    there = pl.ds(pl.multiple_of((1 - c) * HALF, HALF), HALF)
    dims = (((1,), (1,)), ((), ()))
    for span, piece in ((here, own), (there, other)):
        total = lax.dot_general(g0[...], local[span, :], dims, preferred_element_type=F32)
        for d, g in ((1, g1), (2, g2), (3, g3)):
            total += lax.dot_general(g[...], piece[d - 1], dims, preferred_element_type=F32)
        out[:, span] = total.astype(out.dtype)


def backward(where, blocks, own, other, weight, e):
    rows = pl.BlockSpec((HALF, COLS), lambda m, w: (m, 0))
    piece = pl.BlockSpec((3, HALF, COLS), lambda m, w: (0, 0, 0))
    return pl.pallas_call(
        backward_kernel,
        out_shape=jax.ShapeDtypeStruct((ROWS, COLS), BF16),
        grid_spec=pltpu.PrefetchScalarGridSpec(
            num_scalar_prefetch=1,
            grid=(2,),
            in_specs=[rows] * 4
            + [piece, piece, pl.BlockSpec((COLS, COLS), lambda m, w: (w[1 + e], 0))],
            out_specs=pl.BlockSpec((HALF, COLS), lambda m, w: (m, 0)),
        ),
        compiler_params=params(),
        cost_estimate=pl.CostEstimate(
            flops=2 * 512 * 512 * 2048, bytes_accessed=5 << 20, transcendentals=0
        ),
    )(where, *blocks, own, other, weight)


def shift(value, axis, by, size=4):
    return lax.ppermute(value, axis, [(i, (i + by) % size) for i in range(size)])


def flip(value, axis, bit, size=4):
    return lax.ppermute(value, axis, [(i, i ^ bit) for i in range(size)])


def local(
    activations,
    output_gradient,
    frozen_weight,
    adapter_down_factors,
    adapter_up_factors,
    first_moment_down,
    second_moment_down,
    first_moment_up,
    second_moment_up,
    sample_row_prompt,
    majority_vote_reward,
    prompt_adapter_slot,
):
    x, c = lax.axis_index("x"), lax.axis_index("core")
    z, y = lax.axis_index("z"), lax.axis_index("y")
    member = x * 2 + c
    scale_down = WIDTH ** (-0.5)
    scale_up = adapter_scale / RANK**0.5

    received = []
    for d in (1, 2, 3):
        start = lax.rem(z + d, 4) * 2048 + lax.rem(x + y, 4) * COLS + c * HALF
        piece = lax.dynamic_slice_in_dim(frozen_weight, start, HALF, axis=0)
        received.append(shift(piece, "z", d))
    acts = [
        lax.ppermute(
            activations,
            ("x", "y"),
            [(i * 4 + j, i * 4 + (j - i + e) % 4) for i in range(4) for j in range(4)],
        )
        for e in range(4)
    ]
    slots = prompt_adapter_slot
    sent = pick(slots, member[None].astype(jnp.int32), adapter_down_factors, adapter_up_factors)
    adapters = lax.all_to_all(sent, ("x", "core"), 0, 0)
    down = adapters[:, :, 0].reshape(PROMPTS * RANK, COLS)
    up = adapters[:, :, 1].reshape(PROMPTS * RANK, COLS)

    held = slots.reshape(8, PROMPTS)
    mine = (held // PROMPTS == member).astype(jnp.int32)
    turn = jnp.cumsum(mine, axis=1) - 1
    places = jnp.arange(8, dtype=jnp.int32)[:, None] * 2 + turn
    pos = jnp.sum(
        jnp.where(
            held[:, :, None] == member * PROMPTS + jnp.arange(PROMPTS, dtype=jnp.int32),
            places[:, :, None],
            0,
        ),
        axis=(0, 1),
    ).astype(jnp.int32)
    source = lax.dynamic_slice_in_dim(slots, member * PROMPTS, PROMPTS) // PROMPTS
    ids = jnp.arange(PROMPTS, dtype=jnp.int32)
    before = (source[:, None] == source[None, :]) & (ids[:, None] > ids[None, :])
    order = 2 * source + jnp.sum(before.astype(jnp.int32), axis=1)

    labels = sample_row_prompt[0]
    reward = majority_vote_reward[0].astype(F32)
    label = jnp.sum(jnp.where(labels[None, :] == ids[:, None], order[:, None], 0), axis=0)
    onehot = (label[None, :] == ids[:, None]).astype(F32)
    counts = jnp.sum(onehot, axis=1)
    mean_reward = jnp.sum(onehot * reward[None, :], axis=1) / counts
    advantage = reward - jnp.sum(onehot * mean_reward[:, None], axis=0)
    weighted = (advantage[:, None] * output_gradient.astype(F32)).astype(BF16)

    own = [jnp.stack(received)]
    own += [shift(own[0], "x", e) for e in (1, 2, 3)]
    other = [lax.ppermute(piece, "core", [(0, 1), (1, 0)]) for piece in own]
    grads_in = [weighted] + [shift(weighted, "z", d) for d in (1, 2, 3)]

    contract_cols = (((1,), (1,)), ((), ()))
    low_all = lax.dot_general(down, activations, contract_cols, preferred_element_type=F32)
    back_all = lax.dot_general(up, weighted, contract_cols, preferred_element_type=F32)
    low_part = jnp.sum(low_all.reshape(PROMPTS, RANK, ROWS) * onehot[:, None, :], axis=0)
    back_part = jnp.sum(back_all.reshape(PROMPTS, RANK, ROWS) * onehot[:, None, :], axis=0)
    sums = jnp.concatenate([low_part, back_part])
    for axis in ("y", "z"):
        for bit in (1, 2):
            sums = sums + flip(sums, axis, bit)
    low = (scale_down * sums[:RANK]).astype(BF16)
    back_low = (scale_up * sums[RANK:]).astype(BF16)
    half = onehot.astype(BF16)
    low_wide = (half[:, None, :] * low[None, :, :]).reshape(PROMPTS * RANK, ROWS)
    back_wide = (half[:, None, :] * back_low[None, :, :]).reshape(PROMPTS * RANK, ROWS)
    grad_down = scale_down * jnp.dot(back_wide, activations, preferred_element_type=F32)
    grad_up = scale_up * jnp.dot(low_wide, weighted, preferred_element_type=F32)
    grads = jnp.stack(
        [
            grad_down.astype(BF16).reshape(8, 2, RANK, COLS),
            grad_up.astype(BF16).reshape(8, 2, RANK, COLS),
        ],
        axis=2,
    )
    grads = lax.all_to_all(grads, ("x", "core"), 0, 0).reshape(PROMPTS, 2, RANK, COLS)
    updated = adam(
        pos,
        grads,
        adapter_down_factors,
        adapter_up_factors,
        first_moment_down,
        second_moment_down,
        first_moment_up,
        second_moment_up,
    )

    where = jnp.stack([c] + [z * 4 + lax.rem(x + y + 4 - e, 4) for e in range(4)]).astype(jnp.int32)
    input_parts = []
    for e in range(4):
        part = backward(where, grads_in, own[e], other[e], frozen_weight, e)
        input_parts.append(
            lax.ppermute(
                part,
                ("x", "y"),
                [(i * 4 + j, i * 4 + (i + j - e) % 4) for i in range(4) for j in range(4)],
            )
        )
    layer_parts = [
        shift(forward(where, acts, own, other, d), "z", -d) for d in (1, 3, 2)
    ]
    base = forward_local(where, acts, frozen_weight)
    contract_rows = (((0,), (0,)), ((), ()))
    layer = base + scale_up * lax.dot_general(
        low_wide, up, contract_rows, preferred_element_type=F32
    )
    for part in layer_parts:
        layer = layer + part.astype(F32)
    inward = scale_down * lax.dot_general(
        back_wide, down, contract_rows, preferred_element_type=F32
    )
    for part in input_parts:
        inward = inward + part.astype(F32)
    odn, oup, o1d, o2d, o1u, o2u = updated
    return layer.astype(BF16), inward.astype(BF16), odn, oup, o1d, o2d, o1u, o2u


def solution(mesh):
    fine = Mesh(mesh.devices.reshape(4, 2, 4, 4), ("x", "core", "z", "y"))
    grp, tp = ("x", "core"), ("z", "y")
    rows, slab = P(grp, tp), P(grp, None, tp)
    in_specs = (rows, rows, P(None, tp)) + (slab,) * 6 + (P(grp, None), P(grp, None), P())
    out_specs = (rows, rows) + (slab,) * 6
    return jax.shard_map(local, mesh=fine, in_specs=in_specs, out_specs=out_specs, check_vma=False)
```

```python
import functools

import jax
import jax.numpy as jnp
from jax import lax
from jax.experimental import pallas as pl
from jax.experimental.pallas import tpu as pltpu
from jax.sharding import Mesh, PartitionSpec as P

beta_first = 0.9
beta_second = 0.999
step_rate = 0.2
adam_eps = 1e-08
adapter_scale = 2.0

WIDTH = 8192
RANK = 32
COLS = 512
HALF = 256
ROWS = 512
PROMPTS = 16
ANY = pl.BlockSpec(memory_space=pl.ANY)
VMEM = pl.BlockSpec(memory_space=pltpu.VMEM)
F32 = jnp.float32
BF16 = jnp.bfloat16


def params(mib=60):
    return pltpu.CompilerParams(vmem_limit_bytes=mib * 1024 * 1024)


def pick_kernel(slots, member, down, up, out):
    g = member[0]

    def group(d, carry):
        def step(p, j):
            s = slots[d * PROMPTS + p]
            mine = lax.div(s, PROMPTS) == g

            @pl.when(mine)
            def _():
                i = lax.rem(s, PROMPTS)
                out[d * 2 + j, 0] = down[i]
                out[d * 2 + j, 1] = up[i]

            return j + mine.astype(jnp.int32)

        lax.fori_loop(0, PROMPTS, step, jnp.int32(0))
        return carry

    lax.fori_loop(0, 8, group, 0)


def pick(slots, member, down, up):
    return pl.pallas_call(
        pick_kernel,
        out_shape=jax.ShapeDtypeStruct((PROMPTS, 2, RANK, COLS), BF16),
        grid_spec=pltpu.PrefetchScalarGridSpec(
            num_scalar_prefetch=2, grid=(), in_specs=[VMEM, VMEM], out_specs=VMEM
        ),
        compiler_params=params(),
        cost_estimate=pl.CostEstimate(flops=0, bytes_accessed=4 << 20, transcendentals=0),
    )(slots, member, down, up)


def adam_kernel(pos, grads, dn, up, m1d, m2d, m1u, m2u, odn, oup, o1d, o2d, o1u, o2u):
    i0 = pl.program_id(0) * 4
    for k in range(4):
        q = pos[i0 + k]
        for which, (f, m1, m2, of, o1, o2) in enumerate(
            ((dn, m1d, m2d, odn, o1d, o2d), (up, m1u, m2u, oup, o1u, o2u))
        ):
            grad = grads[q, which].astype(F32)
            first = beta_first * m1[k] + (1.0 - beta_first) * grad
            second = beta_second * m2[k] + (1.0 - beta_second) * grad * grad
            of[k] = (
                f[k].astype(F32) - step_rate * first / (jnp.sqrt(second) + adam_eps)
            ).astype(BF16)
            o1[k] = first
            o2[k] = second


def adam(pos, grads, dn, up, m1d, m2d, m1u, m2u):
    block = pl.BlockSpec((4, RANK, COLS), lambda i, pos: (i, 0, 0))
    half = jax.ShapeDtypeStruct((PROMPTS, RANK, COLS), BF16)
    full = jax.ShapeDtypeStruct((PROMPTS, RANK, COLS), F32)
    return pl.pallas_call(
        adam_kernel,
        out_shape=(half, half, full, full, full, full),
        grid_spec=pltpu.PrefetchScalarGridSpec(
            num_scalar_prefetch=1,
            grid=(4,),
            in_specs=[pl.BlockSpec((PROMPTS, 2, RANK, COLS), lambda i, pos: (0, 0, 0, 0))]
            + [block] * 6,
            out_specs=[block] * 6,
        ),
        compiler_params=params(),
        cost_estimate=pl.CostEstimate(flops=8 << 20, bytes_accessed=12 << 20, transcendentals=0),
    )(pos, grads, dn, up, m1d, m2d, m1u, m2u)


def partial_kernel(where, advantage, acts, *refs):
    grads, own, other, weight = refs[0:4], refs[4:8], refs[8:12], refs[12]
    forward, backward = refs[13:17], refs[17:21]
    a_held, g_held, w_held, a_sem, g_sem, w_sem = refs[21:]
    x, c, z, y = (where[i] for i in range(4))

    def span(i):
        return pl.ds(i * COLS, COLS)

    a_loads, g_loads, w_loads = [], [], []
    for i in range(4):
        a_loads.append(
            pltpu.make_async_copy(acts.at[lax.rem(y + i, 4)], a_held.at[:, span(i)], a_sem)
        )
        g_loads.append(pltpu.make_async_copy(grads[i], g_held.at[:, span(i)], g_sem))
    for d in range(4):
        for i in range(4):
            if d == 0:
                first = pl.multiple_of((z * 4 + lax.rem(y + i, 4)) * COLS, COLS)
                copies = [(weight.at[pl.ds(first, COLS)], i * COLS, COLS)]
            else:
                turn = lax.rem(x - i + 4, 4) * COLS
                copies = [
                    (own[i].at[d - 1], turn + c * HALF, HALF),
                    (other[i].at[d - 1], turn + (1 - c) * HALF, HALF),
                ]
            for source, first, length in copies:
                rows = pl.ds(pl.multiple_of(first, HALF), length)
                w_loads.append(
                    pltpu.make_async_copy(source, w_held.at[rows, span(d)], w_sem.at[d])
                )
    local, remote = w_loads[:4], w_loads[4:]
    groups = {0: local, 1: remote[:8], 2: remote[8:16], 3: remote[16:]}
    order = (1, 3, 2, 0)
    for copy in a_loads:
        copy.start()
    for d in order:
        for copy in groups[d]:
            copy.start()
    for copy in g_loads:
        copy.start()
    for copy in a_loads:
        copy.wait()
    for d in order:
        for copy in groups[d]:
            copy.wait()
        forward[d][...] = jnp.dot(
            a_held[...], w_held[:, span(d)], preferred_element_type=F32
        ).astype(BF16)
    for copy in g_loads:
        copy.wait()
    gain = advantage[...]
    for d in range(4):
        g_held[:, span(d)] = (gain * g_held[:, span(d)].astype(F32)).astype(BF16)
    dims = (((1,), (1,)), ((), ()))
    for i in order:
        backward[i][...] = lax.dot_general(
            g_held[...], w_held[span(i)], dims, preferred_element_type=F32
        ).astype(BF16)


def partials(where, advantage, acts, grads, own, other, weight):
    block = jax.ShapeDtypeStruct((ROWS, COLS), BF16)
    outs = pl.pallas_call(
        partial_kernel,
        out_shape=[block] * 8,
        grid_spec=pltpu.PrefetchScalarGridSpec(
            num_scalar_prefetch=1,
            grid=(),
            in_specs=[VMEM] + [ANY] * 14,
            out_specs=[VMEM] * 8,
            scratch_shapes=[
                pltpu.VMEM((ROWS, 4 * COLS), BF16),
                pltpu.VMEM((ROWS, 4 * COLS), BF16),
                pltpu.VMEM((4 * COLS, 4 * COLS), BF16),
                pltpu.SemaphoreType.DMA(()),
                pltpu.SemaphoreType.DMA(()),
                pltpu.SemaphoreType.DMA((4,)),
            ],
        ),
        compiler_params=params(),
        cost_estimate=pl.CostEstimate(
            flops=4 * 512 * 2048 * 2048, bytes_accessed=16 << 20, transcendentals=0
        ),
    )(where, advantage, acts, *grads, *own, *other, weight)
    return outs[:4], outs[4:]


def shift(value, axis, by, size=4):
    return lax.ppermute(value, axis, [(i, (i + by) % size) for i in range(size)])


def flip(value, axis, bit, size=4):
    return lax.ppermute(value, axis, [(i, i ^ bit) for i in range(size)])


def local(
    activations,
    output_gradient,
    frozen_weight,
    adapter_down_factors,
    adapter_up_factors,
    first_moment_down,
    second_moment_down,
    first_moment_up,
    second_moment_up,
    sample_row_prompt,
    majority_vote_reward,
    prompt_adapter_slot,
):
    x, c = lax.axis_index("x"), lax.axis_index("core")
    z, y = lax.axis_index("z"), lax.axis_index("y")
    member = x * 2 + c
    scale_down = WIDTH ** (-0.5)
    scale_up = adapter_scale / RANK**0.5

    acts = lax.all_gather(activations, "y", axis=0)
    parts = []
    source = frozen_weight
    for turn in (0, 2):
        received = []
        for d in (1, 2, 3):
            start = lax.rem(z + d, 4) * 2048 + lax.rem(x + y + turn, 4) * COLS + c * HALF
            piece = lax.dynamic_slice_in_dim(source, start, HALF, axis=0)
            received.append(shift(piece, "z", d))
        parts.append(jnp.stack(received))
        parts[0], source = lax.optimization_barrier((parts[0], frozen_weight))
    grad, pieces = lax.optimization_barrier((output_gradient, parts[1]))
    parts[1] = pieces
    grads_in = [output_gradient] + [shift(grad, "z", d) for d in (1, 2, 3)]
    slots = prompt_adapter_slot
    sent = pick(slots, member[None].astype(jnp.int32), adapter_down_factors, adapter_up_factors)
    adapters = lax.all_to_all(sent.reshape(8, 2, 2, RANK, COLS), ("x", "core"), 0, 0)
    adapters, parts[0] = lax.optimization_barrier((adapters, parts[0]))
    down = adapters[:, :, 0].reshape(PROMPTS * RANK, COLS)
    up = adapters[:, :, 1].reshape(PROMPTS * RANK, COLS)

    held = slots.reshape(8, PROMPTS)
    mine = (held // PROMPTS == member).astype(jnp.int32)
    turn = jnp.cumsum(mine, axis=1) - 1
    places = jnp.arange(8, dtype=jnp.int32)[:, None] * 2 + turn
    pos = jnp.sum(
        jnp.where(
            held[:, :, None] == member * PROMPTS + jnp.arange(PROMPTS, dtype=jnp.int32),
            places[:, :, None],
            0,
        ),
        axis=(0, 1),
    ).astype(jnp.int32)
    source = lax.dynamic_slice_in_dim(slots, member * PROMPTS, PROMPTS) // PROMPTS
    ids = jnp.arange(PROMPTS, dtype=jnp.int32)
    before = (source[:, None] == source[None, :]) & (ids[:, None] > ids[None, :])
    order = 2 * source + jnp.sum(before.astype(jnp.int32), axis=1)

    labels = sample_row_prompt[0]
    reward = majority_vote_reward[0].astype(F32)
    label = jnp.sum(jnp.where(labels[None, :] == ids[:, None], order[:, None], 0), axis=0)
    onehot = (label[None, :] == ids[:, None]).astype(F32)
    counts = jnp.sum(onehot, axis=1)
    mean_reward = jnp.sum(onehot * reward[None, :], axis=1) / counts
    advantage = reward - jnp.sum(onehot * mean_reward[:, None], axis=0)
    weighted = (advantage[:, None] * output_gradient.astype(F32)).astype(BF16)

    own = [parts[0], shift(parts[0], "x", 1), parts[1], shift(parts[0], "x", 3)]
    other = [lax.ppermute(piece, "core", [(0, 1), (1, 0)]) for piece in own]

    contract_cols = (((1,), (1,)), ((), ()))
    low_all = lax.dot_general(down, activations, contract_cols, preferred_element_type=F32)
    back_all = lax.dot_general(up, weighted, contract_cols, preferred_element_type=F32)
    low_part = jnp.sum(low_all.reshape(PROMPTS, RANK, ROWS) * onehot[:, None, :], axis=0)
    back_part = jnp.sum(back_all.reshape(PROMPTS, RANK, ROWS) * onehot[:, None, :], axis=0)
    sums = jnp.concatenate([low_part, back_part])
    for axis in ("y", "z"):
        for bit in (1, 2):
            sums = sums + flip(sums, axis, bit)
    low = (scale_down * sums[:RANK]).astype(BF16)
    back_low = (scale_up * sums[RANK:]).astype(BF16)
    half = onehot.astype(BF16)
    low_wide = (half[:, None, :] * low[None, :, :]).reshape(PROMPTS * RANK, ROWS)
    back_wide = (half[:, None, :] * back_low[None, :, :]).reshape(PROMPTS * RANK, ROWS)
    grad_down = scale_down * jnp.dot(back_wide, activations, preferred_element_type=F32)
    grad_up = scale_up * jnp.dot(low_wide, weighted, preferred_element_type=F32)
    grads = jnp.stack(
        [
            grad_down.astype(BF16).reshape(8, 2, RANK, COLS),
            grad_up.astype(BF16).reshape(8, 2, RANK, COLS),
        ],
        axis=2,
    )
    grads = lax.all_to_all(grads, ("x", "core"), 0, 0).reshape(PROMPTS, 2, RANK, COLS)
    updated = adam(
        pos,
        grads,
        adapter_down_factors,
        adapter_up_factors,
        first_moment_down,
        second_moment_down,
        first_moment_up,
        second_moment_up,
    )

    where = jnp.stack([x, c, z, y]).astype(jnp.int32)
    layer_parts, input_parts = partials(
        where, advantage[:, None], acts, grads_in, own, other, frozen_weight
    )
    layer_parts = [layer_parts[0]] + [shift(layer_parts[d], "z", -d) for d in (1, 3, 2)]
    input_parts = [input_parts[0]] + [shift(input_parts[o], "y", o) for o in (1, 3, 2)]
    contract_rows = (((0,), (0,)), ((), ()))
    layer = scale_up * lax.dot_general(low_wide, up, contract_rows, preferred_element_type=F32)
    for part in layer_parts:
        layer = layer + part.astype(F32)
    inward = scale_down * lax.dot_general(
        back_wide, down, contract_rows, preferred_element_type=F32
    )
    for part in input_parts:
        inward = inward + part.astype(F32)
    odn, oup, o1d, o2d, o1u, o2u = updated
    return layer.astype(BF16), inward.astype(BF16), odn, oup, o1d, o2d, o1u, o2u


def solution(mesh):
    fine = Mesh(mesh.devices.reshape(4, 2, 4, 4), ("x", "core", "z", "y"))
    grp, tp = ("x", "core"), ("z", "y")
    rows, slab = P(grp, tp), P(grp, None, tp)
    in_specs = (rows, rows, P(None, tp)) + (slab,) * 6 + (P(grp, None), P(grp, None), P())
    out_specs = (rows, rows) + (slab,) * 6
    return jax.shard_map(local, mesh=fine, in_specs=in_specs, out_specs=out_specs, check_vma=False)
```

```python
import functools

import jax
import jax.numpy as jnp
from jax import lax
from jax.experimental import pallas as pl
from jax.experimental.pallas import tpu as pltpu
from jax.sharding import Mesh, PartitionSpec as P

beta_first = 0.9
beta_second = 0.999
step_rate = 0.2
adam_eps = 1e-08
adapter_scale = 2.0

WIDTH = 8192
RANK = 32
COLS = 512
HALF = 256
ROWS = 512
PROMPTS = 16
ANY = pl.BlockSpec(memory_space=pl.ANY)
VMEM = pl.BlockSpec(memory_space=pltpu.VMEM)
F32 = jnp.float32
BF16 = jnp.bfloat16


def params(mib=60):
    return pltpu.CompilerParams(vmem_limit_bytes=mib * 1024 * 1024)


def pick_kernel(slots, member, down, up, out, pos):
    g = member[0]

    def group(d, carry):
        def step(p, j):
            s = slots[d * PROMPTS + p]
            mine = lax.div(s, PROMPTS) == g

            @pl.when(mine)
            def _():
                i = lax.rem(s, PROMPTS)
                pos[i] = d * 2 + j
                out[d * 2 + j, 0] = down[i]
                out[d * 2 + j, 1] = up[i]

            return j + mine.astype(jnp.int32)

        lax.fori_loop(0, PROMPTS, step, jnp.int32(0))
        return carry

    lax.fori_loop(0, 8, group, 0)


def pick(slots, member, down, up):
    small = jax.ShapeDtypeStruct((PROMPTS,), jnp.int32)
    smem = pl.BlockSpec(memory_space=pltpu.SMEM)
    return pl.pallas_call(
        pick_kernel,
        out_shape=(jax.ShapeDtypeStruct((PROMPTS, 2, RANK, COLS), BF16), small),
        grid_spec=pltpu.PrefetchScalarGridSpec(
            num_scalar_prefetch=2,
            grid=(),
            in_specs=[VMEM, VMEM],
            out_specs=(VMEM, smem),
        ),
        compiler_params=params(),
        cost_estimate=pl.CostEstimate(flops=1, bytes_accessed=1, transcendentals=0),
    )(slots, member, down, up)


def adam_kernel(pos, grads, dn, up, m1d, m2d, m1u, m2u, odn, oup, o1d, o2d, o1u, o2u):
    i0 = pl.program_id(0) * 4
    for k in range(4):
        q = pos[i0 + k]
        for which, (f, m1, m2, of, o1, o2) in enumerate(
            ((dn, m1d, m2d, odn, o1d, o2d), (up, m1u, m2u, oup, o1u, o2u))
        ):
            grad = grads[q, which].astype(F32)
            first = beta_first * m1[k] + (1.0 - beta_first) * grad
            second = beta_second * m2[k] + (1.0 - beta_second) * grad * grad
            of[k] = (
                f[k].astype(F32) - step_rate * first / (jnp.sqrt(second) + adam_eps)
            ).astype(BF16)
            o1[k] = first
            o2[k] = second


def adam(pos, grads, dn, up, m1d, m2d, m1u, m2u):
    block = pl.BlockSpec((4, RANK, COLS), lambda i, pos: (i, 0, 0))
    half = jax.ShapeDtypeStruct((PROMPTS, RANK, COLS), BF16)
    full = jax.ShapeDtypeStruct((PROMPTS, RANK, COLS), F32)
    return pl.pallas_call(
        adam_kernel,
        out_shape=(half, half, full, full, full, full),
        grid_spec=pltpu.PrefetchScalarGridSpec(
            num_scalar_prefetch=1,
            grid=(4,),
            in_specs=[pl.BlockSpec((PROMPTS, 2, RANK, COLS), lambda i, pos: (0, 0, 0, 0))]
            + [block] * 6,
            out_specs=[block] * 6,
        ),
        compiler_params=params(),
        cost_estimate=pl.CostEstimate(flops=1, bytes_accessed=1, transcendentals=0),
    )(pos, grads, dn, up, m1d, m2d, m1u, m2u)


def partial_kernel(where, *refs):
    acts, grads, own, other, weight = refs[0], refs[1:5], refs[5:9], refs[9:13], refs[13]
    forward, backward = refs[14:18], refs[18:22]
    a_held, g_held, w_held, o_held, a_sem, g_sem, w_sem, o_sem = refs[22:]
    x, c, z, y = (where[i] for i in range(4))

    def span(i):
        return pl.ds(i * COLS, COLS)

    a_loads, g_loads, w_loads = [], [], []
    for i in range(4):
        a_loads.append(
            pltpu.make_async_copy(acts.at[lax.rem(y + i, 4)], a_held.at[:, span(i)], a_sem)
        )
        g_loads.append(pltpu.make_async_copy(grads[i], g_held.at[:, span(i)], g_sem))
    for d in range(4):
        for i in range(4):
            if d == 0:
                first = pl.multiple_of((z * 4 + lax.rem(y + i, 4)) * COLS, COLS)
                copies = [(weight.at[pl.ds(first, COLS)], i * COLS, COLS)]
            else:
                turn = lax.rem(x - i + 4, 4) * COLS
                copies = [
                    (own[i].at[d - 1], turn + c * HALF, HALF),
                    (other[i].at[d - 1], turn + (1 - c) * HALF, HALF),
                ]
            for source, first, length in copies:
                rows = pl.ds(pl.multiple_of(first, HALF), length)
                w_loads.append(
                    pltpu.make_async_copy(source, w_held.at[rows, span(d)], w_sem.at[d])
                )
    local, remote = w_loads[:4], w_loads[4:]
    groups = {0: local, 1: remote[:8], 2: remote[8:16], 3: remote[16:]}
    order = (1, 3, 2, 0)
    for copy in a_loads:
        copy.start()
    for d in order:
        for copy in groups[d]:
            copy.start()
    for copy in g_loads:
        copy.start()
    for copy in a_loads:
        copy.wait()
    for d in order:
        for copy in groups[d]:
            copy.wait()
        o_held[d] = jnp.dot(
            a_held[...], w_held[:, span(d)], preferred_element_type=F32
        ).astype(BF16)
        pltpu.make_async_copy(o_held.at[d], forward[d], o_sem.at[d]).start()
    for copy in g_loads:
        copy.wait()
    dims = (((1,), (1,)), ((), ()))
    for i in order:
        o_held[4 + i] = lax.dot_general(
            g_held[...], w_held[span(i)], dims, preferred_element_type=F32
        ).astype(BF16)
        pltpu.make_async_copy(o_held.at[4 + i], backward[i], o_sem.at[4 + i]).start()
    for i in range(4):
        pltpu.make_async_copy(o_held.at[i], forward[i], o_sem.at[i]).wait()
        pltpu.make_async_copy(o_held.at[4 + i], backward[i], o_sem.at[4 + i]).wait()


def partials(where, acts, grads, own, other, weight):
    block = jax.ShapeDtypeStruct((ROWS, COLS), BF16)
    outs = pl.pallas_call(
        partial_kernel,
        out_shape=[block] * 8,
        grid_spec=pltpu.PrefetchScalarGridSpec(
            num_scalar_prefetch=1,
            grid=(),
            in_specs=[ANY] * 14,
            out_specs=[ANY] * 8,
            scratch_shapes=[
                pltpu.VMEM((ROWS, 4 * COLS), BF16),
                pltpu.VMEM((ROWS, 4 * COLS), BF16),
                pltpu.VMEM((4 * COLS, 4 * COLS), BF16),
                pltpu.VMEM((8, ROWS, COLS), BF16),
                pltpu.SemaphoreType.DMA(()),
                pltpu.SemaphoreType.DMA(()),
                pltpu.SemaphoreType.DMA((4,)),
                pltpu.SemaphoreType.DMA((8,)),
            ],
        ),
        compiler_params=params(),
        cost_estimate=pl.CostEstimate(flops=1, bytes_accessed=1, transcendentals=0),
    )(where, acts, *grads, *own, *other, weight)
    return outs[:4], outs[4:]


def shift(value, axis, by, size=4):
    return lax.ppermute(value, axis, [(i, (i + by) % size) for i in range(size)])


def flip(value, axis, bit, size=4):
    return lax.ppermute(value, axis, [(i, i ^ bit) for i in range(size)])


def local(
    activations,
    output_gradient,
    frozen_weight,
    adapter_down_factors,
    adapter_up_factors,
    first_moment_down,
    second_moment_down,
    first_moment_up,
    second_moment_up,
    sample_row_prompt,
    majority_vote_reward,
    prompt_adapter_slot,
):
    x, c = lax.axis_index("x"), lax.axis_index("core")
    z, y = lax.axis_index("z"), lax.axis_index("y")
    member = x * 2 + c
    scale_down = WIDTH ** (-0.5)
    scale_up = adapter_scale / RANK**0.5

    cuts = [
        [
            lax.dynamic_slice_in_dim(
                frozen_weight,
                lax.rem(z + d, 4) * 2048 + lax.rem(x + y + turn, 4) * COLS + c * HALF,
                HALF,
                axis=0,
            )
            for d in (1, 2, 3)
        ]
        for turn in (0, 2)
    ]
    first = {d: shift(cut, "z", d) for d, cut in zip((1, 2, 3), cuts[0])}
    second = {d: shift(cuts[1][d - 1], "z", d) for d in (1, 3)}
    near = jnp.stack([first[d] for d in (1, 2, 3)])
    cut, _ = lax.optimization_barrier((cuts[1][1], first))
    second[2] = shift(cut, "z", 2)
    far = jnp.stack([second[d] for d in (1, 2, 3)])
    sent, _ = lax.optimization_barrier((near, (second[1], second[3])))
    own = [near, shift(sent, "x", 1), far, shift(sent, "x", 3)]
    other = [lax.ppermute(piece, "core", [(0, 1), (1, 0)]) for piece in own]
    slots = prompt_adapter_slot
    slots, _ = lax.optimization_barrier((slots, cuts[0]))
    sent, pos = pick(
        slots, member[None].astype(jnp.int32), adapter_down_factors, adapter_up_factors
    )
    adapters = lax.all_to_all(sent.reshape(8, 2, 2, RANK, COLS), ("x", "core"), 0, 0)
    adapters, _ = lax.optimization_barrier((adapters, (near, second[1], second[3])))
    act, _ = lax.optimization_barrier((activations, adapters))
    acts = lax.all_to_all(jnp.broadcast_to(act[None], (4, ROWS, COLS)), "y", 0, 0)
    down = adapters[:, :, 0].reshape(PROMPTS * RANK, COLS)
    up = adapters[:, :, 1].reshape(PROMPTS * RANK, COLS)

    source = lax.dynamic_slice_in_dim(slots, member * PROMPTS, PROMPTS) // PROMPTS
    ids = jnp.arange(PROMPTS, dtype=jnp.int32)
    before = (source[:, None] == source[None, :]) & (ids[:, None] > ids[None, :])
    order = 2 * source + jnp.sum(before.astype(jnp.int32), axis=1)
    labels = sample_row_prompt[0]
    reward = majority_vote_reward[0].astype(F32)
    label = jnp.sum(jnp.where(labels[None, :] == ids[:, None], order[:, None], 0), axis=0)
    onehot = (label[None, :] == ids[:, None]).astype(F32)
    counts = jnp.sum(onehot, axis=1)
    mean_reward = jnp.sum(onehot * reward[None, :], axis=1) / counts
    advantage = reward - jnp.sum(onehot * mean_reward[:, None], axis=0)
    weighted = (advantage[:, None] * output_gradient.astype(F32)).astype(BF16)

    grads_in = {0: weighted}
    sent, _ = lax.optimization_barrier((weighted, second[2]))
    grads_in[1], grads_in[3] = shift(sent, "z", 1), shift(sent, "z", 3)
    sent, _ = lax.optimization_barrier((weighted, (grads_in[1], grads_in[3])))
    grads_in[2] = shift(sent, "z", 2)

    contract_cols = (((1,), (1,)), ((), ()))
    low_all = lax.dot_general(down, activations, contract_cols, preferred_element_type=F32)
    back_all = lax.dot_general(up, weighted, contract_cols, preferred_element_type=F32)
    low_part = jnp.sum(low_all.reshape(PROMPTS, RANK, ROWS) * onehot[:, None, :], axis=0)
    back_part = jnp.sum(back_all.reshape(PROMPTS, RANK, ROWS) * onehot[:, None, :], axis=0)
    sums = jnp.concatenate([low_part, back_part])
    sums = sums + sum(shift(sums, "z", i) for i in (1, 3, 2))
    sums, _ = lax.optimization_barrier((sums, (own[1], own[3], other[0], other[2], grads_in[1], grads_in[3], acts)))
    sums = sums + sum(shift(sums, "y", i) for i in (1, 3, 2))
    low = (scale_down * sums[:RANK]).astype(BF16)
    back_low = (scale_up * sums[RANK:]).astype(BF16)
    half = onehot.astype(BF16)
    low_wide = (half[:, None, :] * low[None, :, :]).reshape(PROMPTS * RANK, ROWS)
    back_wide = (half[:, None, :] * back_low[None, :, :]).reshape(PROMPTS * RANK, ROWS)
    where = jnp.stack([x, c, z, y]).astype(jnp.int32)
    layer_parts, input_parts = partials(
        where, acts, [grads_in[i] for i in range(4)], own, other, frozen_weight
    )
    layer_parts = {d: shift(layer_parts[d], "z", -d) if d else layer_parts[d] for d in (1, 3, 2, 0)}
    input_parts = {o: shift(input_parts[o], "y", o) if o else input_parts[o] for o in (1, 3, 2, 0)}
    grad_down = scale_down * jnp.dot(back_wide, activations, preferred_element_type=F32)
    grad_up = scale_up * jnp.dot(low_wide, weighted, preferred_element_type=F32)
    grads = jnp.stack(
        [
            grad_down.astype(BF16).reshape(8, 2, RANK, COLS),
            grad_up.astype(BF16).reshape(8, 2, RANK, COLS),
        ],
        axis=2,
    )
    grads = lax.all_to_all(grads, ("x", "core"), 0, 0).reshape(PROMPTS, 2, RANK, COLS)
    grads, _ = lax.optimization_barrier((grads, layer_parts[1]))
    updated = adam(
        pos,
        grads,
        adapter_down_factors,
        adapter_up_factors,
        first_moment_down,
        second_moment_down,
        first_moment_up,
        second_moment_up,
    )

    contract_rows = (((0,), (0,)), ((), ()))
    layer = layer_parts[0].astype(F32) + scale_up * lax.dot_general(
        low_wide, up, contract_rows, preferred_element_type=F32
    )
    inward = input_parts[0].astype(F32) + scale_down * lax.dot_general(
        back_wide, down, contract_rows, preferred_element_type=F32
    )
    inward, updated = lax.optimization_barrier((inward, updated))
    layer = lax.optimization_barrier(layer)
    for i in (1, 3, 2):
        layer = layer + layer_parts[i].astype(F32)
        inward = inward + input_parts[i].astype(F32)
    odn, oup, o1d, o2d, o1u, o2u = updated
    return layer.astype(BF16), inward.astype(BF16), odn, oup, o1d, o2d, o1u, o2u


def solution(mesh):
    fine = Mesh(mesh.devices.reshape(4, 2, 4, 4), ("x", "core", "z", "y"))
    grp, tp = ("x", "core"), ("z", "y")
    rows, slab = P(grp, tp), P(grp, None, tp)
    in_specs = (rows, rows, P(None, tp)) + (slab,) * 6 + (P(grp, None), P(grp, None), P())
    out_specs = (rows, rows) + (slab,) * 6
    return jax.shard_map(local, mesh=fine, in_specs=in_specs, out_specs=out_specs, check_vma=False)
```

```python
import functools

import jax
import jax.numpy as jnp
from jax import lax
from jax.experimental import pallas as pl
from jax.experimental.pallas import tpu as pltpu
from jax.sharding import Mesh, PartitionSpec as P

beta_first = 0.9
beta_second = 0.999
step_rate = 0.2
adam_eps = 1e-08
adapter_scale = 2.0

WIDTH = 8192
RANK = 32
COLS = 512
HALF = 256
ROWS = 512
PROMPTS = 16
ANY = pl.BlockSpec(memory_space=pl.ANY)
VMEM = pl.BlockSpec(memory_space=pltpu.VMEM)
F32 = jnp.float32
BF16 = jnp.bfloat16


def params(mib=60):
    return pltpu.CompilerParams(vmem_limit_bytes=mib * 1024 * 1024)


def pick_kernel(slots, member, down, up, out, pos):
    g = member[0]

    def group(d, carry):
        def step(p, j):
            s = slots[d * PROMPTS + p]
            mine = lax.div(s, PROMPTS) == g

            @pl.when(mine)
            def _():
                i = lax.rem(s, PROMPTS)
                pos[i] = d * 2 + j
                out[d * 2 + j, 0] = down[i]
                out[d * 2 + j, 1] = up[i]

            return j + mine.astype(jnp.int32)

        lax.fori_loop(0, PROMPTS, step, jnp.int32(0), unroll=True)
        return carry

    lax.fori_loop(0, 8, group, 0)


def pick(slots, member, down, up):
    small = jax.ShapeDtypeStruct((PROMPTS,), jnp.int32)
    smem = pl.BlockSpec(memory_space=pltpu.SMEM)
    return pl.pallas_call(
        pick_kernel,
        out_shape=(jax.ShapeDtypeStruct((PROMPTS, 2, RANK, COLS), BF16), small),
        grid_spec=pltpu.PrefetchScalarGridSpec(
            num_scalar_prefetch=2,
            grid=(),
            in_specs=[VMEM, VMEM],
            out_specs=(VMEM, smem),
        ),
        compiler_params=params(),
        cost_estimate=pl.CostEstimate(flops=1, bytes_accessed=1, transcendentals=0),
    )(slots, member, down, up)


def adam_kernel(pos, grads, dn, up, m1d, m2d, m1u, m2u, odn, oup, o1d, o2d, o1u, o2u):
    i0 = pl.program_id(0) * 4
    for k in range(4):
        q = pos[i0 + k]
        for which, (f, m1, m2, of, o1, o2) in enumerate(
            ((dn, m1d, m2d, odn, o1d, o2d), (up, m1u, m2u, oup, o1u, o2u))
        ):
            grad = grads[q, which].astype(F32)
            first = beta_first * m1[k] + (1.0 - beta_first) * grad
            second = beta_second * m2[k] + (1.0 - beta_second) * grad * grad
            of[k] = (
                f[k].astype(F32) - step_rate * first / (jnp.sqrt(second) + adam_eps)
            ).astype(BF16)
            o1[k] = first
            o2[k] = second


def adam(pos, grads, dn, up, m1d, m2d, m1u, m2u):
    block = pl.BlockSpec((4, RANK, COLS), lambda i, pos: (i, 0, 0))
    half = jax.ShapeDtypeStruct((PROMPTS, RANK, COLS), BF16)
    full = jax.ShapeDtypeStruct((PROMPTS, RANK, COLS), F32)
    return pl.pallas_call(
        adam_kernel,
        out_shape=(half, half, full, full, full, full),
        grid_spec=pltpu.PrefetchScalarGridSpec(
            num_scalar_prefetch=1,
            grid=(4,),
            in_specs=[pl.BlockSpec((PROMPTS, 2, RANK, COLS), lambda i, pos: (0, 0, 0, 0))]
            + [block] * 6,
            out_specs=[block] * 6,
        ),
        compiler_params=params(),
        cost_estimate=pl.CostEstimate(flops=1, bytes_accessed=1, transcendentals=0),
    )(pos, grads, dn, up, m1d, m2d, m1u, m2u)


def partial_kernel(where, *refs):
    acts, grads, own, other, weight = refs[0], refs[1:5], refs[5:9], refs[9:13], refs[13]
    forward, backward = refs[14:18], refs[18:22]
    a_held, g_held, w_held, o_held, a_sem, g_sem, w_sem, o_sem = refs[22:]
    x, c, z, y = (where[i] for i in range(4))

    def span(i):
        return pl.ds(i * COLS, COLS)

    a_loads, g_loads, w_loads = [], [], []
    for i in range(4):
        a_loads.append(
            pltpu.make_async_copy(acts.at[lax.rem(y + i, 4)], a_held.at[:, span(i)], a_sem)
        )
        g_loads.append(pltpu.make_async_copy(grads[i], g_held.at[:, span(i)], g_sem))
    for d in range(4):
        for i in range(4):
            if d == 0:
                first = pl.multiple_of((z * 4 + lax.rem(y + i, 4)) * COLS, COLS)
                copies = [(weight.at[pl.ds(first, COLS)], i * COLS, COLS)]
            else:
                turn = lax.rem(x - i + 4, 4) * COLS
                copies = [
                    (own[i].at[d - 1], turn + c * HALF, HALF),
                    (other[i].at[d - 1], turn + (1 - c) * HALF, HALF),
                ]
            for source, first, length in copies:
                rows = pl.ds(pl.multiple_of(first, HALF), length)
                w_loads.append(
                    pltpu.make_async_copy(source, w_held.at[rows, span(d)], w_sem.at[d])
                )
    local, remote = w_loads[:4], w_loads[4:]
    groups = {0: local, 1: remote[:8], 2: remote[8:16], 3: remote[16:]}
    order = (1, 3, 2, 0)
    for copy in a_loads:
        copy.start()
    for d in order:
        for copy in groups[d]:
            copy.start()
    for copy in g_loads:
        copy.start()
    for copy in a_loads:
        copy.wait()
    for d in order:
        for copy in groups[d]:
            copy.wait()
        o_held[d] = jnp.dot(
            a_held[...], w_held[:, span(d)], preferred_element_type=F32
        ).astype(BF16)
        pltpu.make_async_copy(o_held.at[d], forward[d], o_sem.at[d]).start()
    for copy in g_loads:
        copy.wait()
    dims = (((1,), (1,)), ((), ()))
    for i in order:
        o_held[4 + i] = lax.dot_general(
            g_held[...], w_held[span(i)], dims, preferred_element_type=F32
        ).astype(BF16)
        pltpu.make_async_copy(o_held.at[4 + i], backward[i], o_sem.at[4 + i]).start()
    for i in range(4):
        pltpu.make_async_copy(o_held.at[i], forward[i], o_sem.at[i]).wait()
        pltpu.make_async_copy(o_held.at[4 + i], backward[i], o_sem.at[4 + i]).wait()


def partials(where, acts, grads, own, other, weight):
    block = jax.ShapeDtypeStruct((ROWS, COLS), BF16)
    outs = pl.pallas_call(
        partial_kernel,
        out_shape=[block] * 8,
        grid_spec=pltpu.PrefetchScalarGridSpec(
            num_scalar_prefetch=1,
            grid=(),
            in_specs=[ANY] * 14,
            out_specs=[ANY] * 8,
            scratch_shapes=[
                pltpu.VMEM((ROWS, 4 * COLS), BF16),
                pltpu.VMEM((ROWS, 4 * COLS), BF16),
                pltpu.VMEM((4 * COLS, 4 * COLS), BF16),
                pltpu.VMEM((8, ROWS, COLS), BF16),
                pltpu.SemaphoreType.DMA(()),
                pltpu.SemaphoreType.DMA(()),
                pltpu.SemaphoreType.DMA((4,)),
                pltpu.SemaphoreType.DMA((8,)),
            ],
        ),
        compiler_params=params(),
        cost_estimate=pl.CostEstimate(flops=1, bytes_accessed=1, transcendentals=0),
    )(where, acts, *grads, *own, *other, weight)
    return outs[:4], outs[4:]


def grads_kernel(scale_down, scale_up, t0, t1, t2, t3, hot, acts, weighted, out, low_wide, back_wide):
    sums = (t0[...] + t1[...]) + (t2[...] + t3[...])
    low = (scale_down * sums[:RANK]).astype(BF16)
    back = (scale_up * sums[RANK:]).astype(BF16)
    for p in range(PROMPTS):
        rows = pl.ds(p * RANK, RANK)
        low_wide[rows] = hot[p : p + 1, :] * low
        back_wide[rows] = hot[p : p + 1, :] * back
    for which, (scale, wide, other) in enumerate(
        ((scale_down, back_wide, acts), (scale_up, low_wide, weighted))
    ):
        grad = scale * jnp.dot(wide[...], other[...], preferred_element_type=F32)
        out[:, which] = grad.astype(BF16).reshape(PROMPTS, RANK, COLS)


def adapter_grads(terms, hot, acts, weighted, scale_down, scale_up):
    wide = jax.ShapeDtypeStruct((PROMPTS * RANK, ROWS), BF16)
    return pl.pallas_call(
        functools.partial(grads_kernel, scale_down, scale_up),
        out_shape=(jax.ShapeDtypeStruct((PROMPTS, 2, RANK, COLS), BF16), wide, wide),
        in_specs=[VMEM] * 7,
        out_specs=(VMEM,) * 3,
        compiler_params=params(),
        cost_estimate=pl.CostEstimate(flops=1, bytes_accessed=1, transcendentals=0),
    )(*terms, hot, acts, weighted)


def shift(value, axis, by, size=4):
    return lax.ppermute(value, axis, [(i, (i + by) % size) for i in range(size)])


def flip(value, axis, bit, size=4):
    return lax.ppermute(value, axis, [(i, i ^ bit) for i in range(size)])


def local(
    activations,
    output_gradient,
    frozen_weight,
    adapter_down_factors,
    adapter_up_factors,
    first_moment_down,
    second_moment_down,
    first_moment_up,
    second_moment_up,
    sample_row_prompt,
    majority_vote_reward,
    prompt_adapter_slot,
):
    x, c = lax.axis_index("x"), lax.axis_index("core")
    z, y = lax.axis_index("z"), lax.axis_index("y")
    member = x * 2 + c
    scale_down = WIDTH ** (-0.5)
    scale_up = adapter_scale / RANK**0.5

    cuts = [
        [
            lax.dynamic_slice_in_dim(
                frozen_weight,
                lax.rem(z + d, 4) * 2048 + lax.rem(x + y + turn, 4) * COLS + c * HALF,
                HALF,
                axis=0,
            )
            for d in (1, 2, 3)
        ]
        for turn in (0, 2)
    ]
    first = {d: shift(cut, "z", d) for d, cut in zip((1, 2, 3), cuts[0])}
    second = {d: shift(cuts[1][d - 1], "z", d) for d in (1, 3)}
    near = jnp.stack([first[d] for d in (1, 2, 3)])
    cut, _ = lax.optimization_barrier((cuts[1][1], first))
    second[2] = shift(cut, "z", 2)
    far = jnp.stack([second[d] for d in (1, 2, 3)])
    sent, _ = lax.optimization_barrier((near, (second[1], second[3])))
    own = [near, shift(sent, "x", 1), far, shift(sent, "x", 3)]
    other = [lax.ppermute(piece, "core", [(0, 1), (1, 0)]) for piece in own]
    slots = prompt_adapter_slot
    slots, _ = lax.optimization_barrier((slots, cuts[0]))
    sent, pos = pick(
        slots, member[None].astype(jnp.int32), adapter_down_factors, adapter_up_factors
    )
    adapters = lax.all_to_all(sent.reshape(8, 2, 2, RANK, COLS), ("x", "core"), 0, 0)
    adapters, _ = lax.optimization_barrier((adapters, (near, second[1], second[3])))
    act, _ = lax.optimization_barrier((activations, adapters))
    acts = lax.all_to_all(jnp.broadcast_to(act[None], (4, ROWS, COLS)), "y", 0, 0)
    down = adapters[:, :, 0].reshape(PROMPTS * RANK, COLS)
    up = adapters[:, :, 1].reshape(PROMPTS * RANK, COLS)

    source = lax.dynamic_slice_in_dim(slots, member * PROMPTS, PROMPTS) // PROMPTS
    ids = jnp.arange(PROMPTS, dtype=jnp.int32)
    before = (source[:, None] == source[None, :]) & (ids[:, None] > ids[None, :])
    order = 2 * source + jnp.sum(before.astype(jnp.int32), axis=1)
    labels = sample_row_prompt[0]
    reward = majority_vote_reward[0].astype(F32)
    label = jnp.sum(jnp.where(labels[None, :] == ids[:, None], order[:, None], 0), axis=0)
    onehot = (label[None, :] == ids[:, None]).astype(F32)
    counts = jnp.sum(onehot, axis=1)
    mean_reward = jnp.sum(onehot * reward[None, :], axis=1) / counts
    advantage = reward - jnp.sum(onehot * mean_reward[:, None], axis=0)
    weighted = (advantage[:, None] * output_gradient.astype(F32)).astype(BF16)

    sent, _ = lax.optimization_barrier((weighted, second[2]))
    grads_in = {0: weighted} | {d: shift(sent, "z", d) for d in (1, 3, 2)}

    contract_cols = (((1,), (1,)), ((), ()))
    low_all = lax.dot_general(down, activations, contract_cols, preferred_element_type=F32)
    back_all = lax.dot_general(up, weighted, contract_cols, preferred_element_type=F32)
    low_part = jnp.sum(low_all.reshape(PROMPTS, RANK, ROWS) * onehot[:, None, :], axis=0)
    back_part = jnp.sum(back_all.reshape(PROMPTS, RANK, ROWS) * onehot[:, None, :], axis=0)
    sums = jnp.concatenate([low_part, back_part])
    sums, _ = lax.optimization_barrier((sums, other[0]))
    last, _ = lax.optimization_barrier((sums, grads_in))
    sums = (sums + shift(sums, "z", 1)) + (shift(sums, "z", 3) + shift(last, "z", 2))
    sums, _ = lax.optimization_barrier((sums, (own[1], own[3], other[2], acts)))
    terms = [sums] + [shift(sums, "y", i) for i in (1, 3, 2)]
    where = jnp.stack([x, c, z, y]).astype(jnp.int32)
    layer_parts, input_parts = partials(
        where, acts, [grads_in[i] for i in range(4)], own, other, frozen_weight
    )
    layer_parts = {d: shift(layer_parts[d], "z", -d) if d else layer_parts[d] for d in (1, 3, 2, 0)}
    input_parts = {o: shift(input_parts[o], "y", o) if o else input_parts[o] for o in (1, 3, 2, 0)}
    grads, low_wide, back_wide = adapter_grads(
        terms, onehot.astype(BF16), activations, weighted, scale_down, scale_up
    )
    grads = grads.reshape(8, 2, 2, RANK, COLS)
    grads = lax.all_to_all(grads, ("x", "core"), 0, 0).reshape(PROMPTS, 2, RANK, COLS)
    grads, _ = lax.optimization_barrier((grads, layer_parts[1]))
    updated = adam(
        pos,
        grads,
        adapter_down_factors,
        adapter_up_factors,
        first_moment_down,
        second_moment_down,
        first_moment_up,
        second_moment_up,
    )

    contract_rows = (((0,), (0,)), ((), ()))
    layer = layer_parts[0].astype(F32) + scale_up * lax.dot_general(
        low_wide, up, contract_rows, preferred_element_type=F32
    )
    inward = input_parts[0].astype(F32) + scale_down * lax.dot_general(
        back_wide, down, contract_rows, preferred_element_type=F32
    )
    inward, updated = lax.optimization_barrier((inward, updated))
    layer = lax.optimization_barrier(layer)
    for i in (1, 3, 2):
        layer = layer + layer_parts[i].astype(F32)
        inward = inward + input_parts[i].astype(F32)
    odn, oup, o1d, o2d, o1u, o2u = updated
    return layer.astype(BF16), inward.astype(BF16), odn, oup, o1d, o2d, o1u, o2u


def solution(mesh):
    fine = Mesh(mesh.devices.reshape(4, 2, 4, 4), ("x", "core", "z", "y"))
    grp, tp = ("x", "core"), ("z", "y")
    rows, slab = P(grp, tp), P(grp, None, tp)
    in_specs = (rows, rows, P(None, tp)) + (slab,) * 6 + (P(grp, None), P(grp, None), P())
    out_specs = (rows, rows) + (slab,) * 6
    return jax.shard_map(local, mesh=fine, in_specs=in_specs, out_specs=out_specs, check_vma=False)
```

```python
import functools

import jax
import jax.numpy as jnp
from jax import lax
from jax.experimental import pallas as pl
from jax.experimental.pallas import tpu as pltpu
from jax.sharding import Mesh, PartitionSpec as P

beta_first = 0.9
beta_second = 0.999
step_rate = 0.2
adam_eps = 1e-08
adapter_scale = 2.0

WIDTH = 8192
RANK = 32
COLS = 512
HALF = 256
ROWS = 512
PROMPTS = 16
ANY = pl.BlockSpec(memory_space=pl.ANY)
VMEM = pl.BlockSpec(memory_space=pltpu.VMEM)
F32 = jnp.float32
BF16 = jnp.bfloat16


def params(mib=60):
    return pltpu.CompilerParams(vmem_limit_bytes=mib * 1024 * 1024)


def pick_kernel(slots, member, down, up, out, pos):
    g = member[0]

    def group(d, carry):
        def step(p, j):
            s = slots[d * PROMPTS + p]
            mine = lax.div(s, PROMPTS) == g

            @pl.when(mine)
            def _():
                i = lax.rem(s, PROMPTS)
                pos[i] = d * 2 + j
                out[d * 2 + j, 0] = down[i]
                out[d * 2 + j, 1] = up[i]

            return j + mine.astype(jnp.int32)

        lax.fori_loop(0, PROMPTS, step, jnp.int32(0), unroll=True)
        return carry

    lax.fori_loop(0, 8, group, 0)


def pick(slots, member, down, up):
    small = jax.ShapeDtypeStruct((PROMPTS,), jnp.int32)
    smem = pl.BlockSpec(memory_space=pltpu.SMEM)
    return pl.pallas_call(
        pick_kernel,
        out_shape=(jax.ShapeDtypeStruct((PROMPTS, 2, RANK, COLS), BF16), small),
        grid_spec=pltpu.PrefetchScalarGridSpec(
            num_scalar_prefetch=2,
            grid=(),
            in_specs=[VMEM, VMEM],
            out_specs=(VMEM, smem),
        ),
        compiler_params=params(),
        cost_estimate=pl.CostEstimate(flops=1, bytes_accessed=1, transcendentals=0),
    )(slots, member, down, up)


def adam_kernel(pos, grads, dn, up, m1d, m2d, m1u, m2u, odn, oup, o1d, o2d, o1u, o2u):
    i0 = pl.program_id(0) * 4
    for k in range(4):
        q = pos[i0 + k]
        for which, (f, m1, m2, of, o1, o2) in enumerate(
            ((dn, m1d, m2d, odn, o1d, o2d), (up, m1u, m2u, oup, o1u, o2u))
        ):
            grad = grads[q, which].astype(F32)
            first = beta_first * m1[k] + (1.0 - beta_first) * grad
            second = beta_second * m2[k] + (1.0 - beta_second) * grad * grad
            of[k] = (
                f[k].astype(F32) - step_rate * first / (jnp.sqrt(second) + adam_eps)
            ).astype(BF16)
            o1[k] = first
            o2[k] = second


def adam(pos, grads, dn, up, m1d, m2d, m1u, m2u):
    block = pl.BlockSpec((4, RANK, COLS), lambda i, pos: (i, 0, 0))
    half = jax.ShapeDtypeStruct((PROMPTS, RANK, COLS), BF16)
    full = jax.ShapeDtypeStruct((PROMPTS, RANK, COLS), F32)
    return pl.pallas_call(
        adam_kernel,
        out_shape=(half, half, full, full, full, full),
        grid_spec=pltpu.PrefetchScalarGridSpec(
            num_scalar_prefetch=1,
            grid=(4,),
            in_specs=[pl.BlockSpec((PROMPTS, 2, RANK, COLS), lambda i, pos: (0, 0, 0, 0))]
            + [block] * 6,
            out_specs=[block] * 6,
        ),
        compiler_params=params(),
        cost_estimate=pl.CostEstimate(flops=1, bytes_accessed=1, transcendentals=0),
    )(pos, grads, dn, up, m1d, m2d, m1u, m2u)


def partial_kernel(where, *refs):
    acts, grads, own, other, weight = refs[0], refs[1:5], refs[5:9], refs[9:13], refs[13]
    forward, backward = refs[14:18], refs[18:22]
    a_held, g_held, w_held, o_held, a_sem, g_sem, w_sem, o_sem = refs[22:]
    x, c, z, y = (where[i] for i in range(4))

    def span(i):
        return pl.ds(i * COLS, COLS)

    a_loads, g_loads, w_loads = [], [], []
    for i in range(4):
        a_loads.append(
            pltpu.make_async_copy(acts.at[lax.rem(y + i, 4)], a_held.at[:, span(i)], a_sem)
        )
        g_loads.append(pltpu.make_async_copy(grads[i], g_held.at[:, span(i)], g_sem))
    for d in range(4):
        for i in range(4):
            if d == 0:
                first = pl.multiple_of((z * 4 + lax.rem(y + i, 4)) * COLS, COLS)
                copies = [(weight.at[pl.ds(first, COLS)], i * COLS, COLS)]
            else:
                turn = lax.rem(x - i + 4, 4) * COLS
                copies = [
                    (own[i].at[d - 1], turn + c * HALF, HALF),
                    (other[i].at[d - 1], turn + (1 - c) * HALF, HALF),
                ]
            for source, first, length in copies:
                rows = pl.ds(pl.multiple_of(first, HALF), length)
                w_loads.append(
                    pltpu.make_async_copy(source, w_held.at[rows, span(d)], w_sem.at[d])
                )
    local, remote = w_loads[:4], w_loads[4:]
    groups = {0: local, 1: remote[:8], 2: remote[8:16], 3: remote[16:]}
    order = (1, 3, 2, 0)
    for copy in a_loads:
        copy.start()
    for d in order:
        for copy in groups[d]:
            copy.start()
    for copy in g_loads:
        copy.start()
    for copy in a_loads:
        copy.wait()
    for d in order:
        for copy in groups[d]:
            copy.wait()
        o_held[d] = jnp.dot(
            a_held[...], w_held[:, span(d)], preferred_element_type=F32
        ).astype(BF16)
        pltpu.make_async_copy(o_held.at[d], forward[d], o_sem.at[d]).start()
    for copy in g_loads:
        copy.wait()
    dims = (((1,), (1,)), ((), ()))
    for i in order:
        o_held[4 + i] = lax.dot_general(
            g_held[...], w_held[span(i)], dims, preferred_element_type=F32
        ).astype(BF16)
        pltpu.make_async_copy(o_held.at[4 + i], backward[i], o_sem.at[4 + i]).start()
    for i in range(4):
        pltpu.make_async_copy(o_held.at[i], forward[i], o_sem.at[i]).wait()
        pltpu.make_async_copy(o_held.at[4 + i], backward[i], o_sem.at[4 + i]).wait()


def partials(where, acts, grads, own, other, weight):
    block = jax.ShapeDtypeStruct((ROWS, COLS), BF16)
    outs = pl.pallas_call(
        partial_kernel,
        out_shape=[block] * 8,
        grid_spec=pltpu.PrefetchScalarGridSpec(
            num_scalar_prefetch=1,
            grid=(),
            in_specs=[ANY] * 14,
            out_specs=[ANY] * 8,
            scratch_shapes=[
                pltpu.VMEM((ROWS, 4 * COLS), BF16),
                pltpu.VMEM((ROWS, 4 * COLS), BF16),
                pltpu.VMEM((4 * COLS, 4 * COLS), BF16),
                pltpu.VMEM((8, ROWS, COLS), BF16),
                pltpu.SemaphoreType.DMA(()),
                pltpu.SemaphoreType.DMA(()),
                pltpu.SemaphoreType.DMA((4,)),
                pltpu.SemaphoreType.DMA((8,)),
            ],
        ),
        compiler_params=params(),
        cost_estimate=pl.CostEstimate(flops=1, bytes_accessed=1, transcendentals=0),
    )(where, acts, *grads, *own, *other, weight)
    return outs[:4], outs[4:]


def grads_kernel(scale_down, scale_up, t0, t1, t2, t3, hot, acts, weighted, out, low_wide, back_wide):
    sums = (t0[...] + t1[...]) + (t2[...] + t3[...])
    low = (scale_down * sums[:RANK]).astype(BF16)
    back = (scale_up * sums[RANK:]).astype(BF16)
    for p in range(PROMPTS):
        rows = pl.ds(p * RANK, RANK)
        low_wide[rows] = hot[p : p + 1, :] * low
        back_wide[rows] = hot[p : p + 1, :] * back
    for which, (scale, wide, other) in enumerate(
        ((scale_down, back_wide, acts), (scale_up, low_wide, weighted))
    ):
        grad = scale * jnp.dot(wide[...], other[...], preferred_element_type=F32)
        out[:, which] = grad.astype(BF16).reshape(PROMPTS, RANK, COLS)


def adapter_grads(terms, hot, acts, weighted, scale_down, scale_up):
    wide = jax.ShapeDtypeStruct((PROMPTS * RANK, ROWS), BF16)
    return pl.pallas_call(
        functools.partial(grads_kernel, scale_down, scale_up),
        out_shape=(jax.ShapeDtypeStruct((PROMPTS, 2, RANK, COLS), BF16), wide, wide),
        in_specs=[VMEM] * 7,
        out_specs=(VMEM,) * 3,
        compiler_params=params(),
        cost_estimate=pl.CostEstimate(flops=1, bytes_accessed=1, transcendentals=0),
    )(*terms, hot, acts, weighted)


def shift(value, axis, by, size=4):
    return lax.ppermute(value, axis, [(i, (i + by) % size) for i in range(size)])


def flip(value, axis, bit, size=4):
    return lax.ppermute(value, axis, [(i, i ^ bit) for i in range(size)])


def local(
    activations,
    output_gradient,
    frozen_weight,
    adapter_down_factors,
    adapter_up_factors,
    first_moment_down,
    second_moment_down,
    first_moment_up,
    second_moment_up,
    sample_row_prompt,
    majority_vote_reward,
    prompt_adapter_slot,
):
    x, c = lax.axis_index("x"), lax.axis_index("core")
    z, y = lax.axis_index("z"), lax.axis_index("y")
    member = x * 2 + c
    scale_down = WIDTH ** (-0.5)
    scale_up = adapter_scale / RANK**0.5

    cuts = [
        [
            lax.dynamic_slice_in_dim(
                frozen_weight,
                lax.rem(z + d, 4) * 2048 + lax.rem(x + y + turn, 4) * COLS + c * HALF,
                HALF,
                axis=0,
            )
            for d in (1, 2, 3)
        ]
        for turn in (0, 2)
    ]
    first = {d: shift(cut, "z", d) for d, cut in zip((1, 2, 3), cuts[0])}
    second = {d: shift(cuts[1][d - 1], "z", d) for d in (1, 3)}
    near = jnp.stack([first[d] for d in (1, 2, 3)])
    cut, _ = lax.optimization_barrier((cuts[1][1], first))
    second[2] = shift(cut, "z", 2)
    far = jnp.stack([second[d] for d in (1, 2, 3)])
    sent, _ = lax.optimization_barrier((near, (second[1], second[3])))
    own = [near, shift(sent, "x", 1), far, shift(sent, "x", 3)]
    swap = [(0, 1), (1, 0)]
    other = {e: lax.ppermute(own[e], "core", swap) for e in (0, 2)}
    slots = prompt_adapter_slot
    slots, _ = lax.optimization_barrier((slots, cuts[0]))
    sent, pos = pick(
        slots, member[None].astype(jnp.int32), adapter_down_factors, adapter_up_factors
    )
    adapters = lax.all_to_all(sent.reshape(8, 2, 2, RANK, COLS), ("x", "core"), 0, 0)
    adapters, _ = lax.optimization_barrier((adapters, (near, second[1], second[3])))
    act, _ = lax.optimization_barrier((activations, adapters))
    acts = lax.all_to_all(jnp.broadcast_to(act[None], (4, ROWS, COLS)), "y", 0, 0)
    down = adapters[:, :, 0].reshape(PROMPTS * RANK, COLS)
    up = adapters[:, :, 1].reshape(PROMPTS * RANK, COLS)

    source = lax.dynamic_slice_in_dim(slots, member * PROMPTS, PROMPTS) // PROMPTS
    ids = jnp.arange(PROMPTS, dtype=jnp.int32)
    before = (source[:, None] == source[None, :]) & (ids[:, None] > ids[None, :])
    order = 2 * source + jnp.sum(before.astype(jnp.int32), axis=1)
    labels = sample_row_prompt[0]
    reward = majority_vote_reward[0].astype(F32)
    label = jnp.sum(jnp.where(labels[None, :] == ids[:, None], order[:, None], 0), axis=0)
    onehot = (label[None, :] == ids[:, None]).astype(F32)
    counts = jnp.sum(onehot, axis=1)
    mean_reward = jnp.sum(onehot * reward[None, :], axis=1) / counts
    advantage = reward - jnp.sum(onehot * mean_reward[:, None], axis=0)
    weighted = (advantage[:, None] * output_gradient.astype(F32)).astype(BF16)

    sent, _ = lax.optimization_barrier((weighted, second[2]))
    grads_in = {0: weighted} | {d: shift(sent, "z", d) for d in (1, 3, 2)}
    late, _ = lax.optimization_barrier(((own[1], own[3]), (grads_in[1], grads_in[3])))
    other[1], other[3] = (lax.ppermute(piece, "core", swap) for piece in late)
    other = [other[e] for e in range(4)]

    contract_cols = (((1,), (1,)), ((), ()))
    low_all = lax.dot_general(down, activations, contract_cols, preferred_element_type=F32)
    back_all = lax.dot_general(up, weighted, contract_cols, preferred_element_type=F32)
    low_part = jnp.sum(low_all.reshape(PROMPTS, RANK, ROWS) * onehot[:, None, :], axis=0)
    back_part = jnp.sum(back_all.reshape(PROMPTS, RANK, ROWS) * onehot[:, None, :], axis=0)
    sums = jnp.concatenate([low_part, back_part])
    sums, _ = lax.optimization_barrier((sums, other))
    sums = sums + sum(shift(sums, "z", i) for i in (1, 3, 2))
    sums, _ = lax.optimization_barrier((sums, (grads_in, acts)))
    terms = [sums] + [shift(sums, "y", i) for i in (1, 3, 2)]
    where = jnp.stack([x, c, z, y]).astype(jnp.int32)
    layer_parts, input_parts = partials(
        where, acts, [grads_in[i] for i in range(4)], own, other, frozen_weight
    )
    layer_parts = {d: shift(layer_parts[d], "z", -d) if d else layer_parts[d] for d in (1, 3, 2, 0)}
    input_parts = {o: shift(input_parts[o], "y", o) if o else input_parts[o] for o in (1, 3, 2, 0)}
    grads, low_wide, back_wide = adapter_grads(
        terms, onehot.astype(BF16), activations, weighted, scale_down, scale_up
    )
    grads = grads.reshape(8, 2, 2, RANK, COLS)
    grads = lax.all_to_all(grads, ("x", "core"), 0, 0).reshape(PROMPTS, 2, RANK, COLS)
    grads, _ = lax.optimization_barrier((grads, layer_parts[1]))
    updated = adam(
        pos,
        grads,
        adapter_down_factors,
        adapter_up_factors,
        first_moment_down,
        second_moment_down,
        first_moment_up,
        second_moment_up,
    )

    contract_rows = (((0,), (0,)), ((), ()))
    layer = layer_parts[0].astype(F32) + scale_up * lax.dot_general(
        low_wide, up, contract_rows, preferred_element_type=F32
    )
    inward = input_parts[0].astype(F32) + scale_down * lax.dot_general(
        back_wide, down, contract_rows, preferred_element_type=F32
    )
    layer, inward = lax.optimization_barrier((layer, inward))
    for i in (1, 3, 2):
        layer = layer + layer_parts[i].astype(F32)
        inward = inward + input_parts[i].astype(F32)
    odn, oup, o1d, o2d, o1u, o2u = updated
    return layer.astype(BF16), inward.astype(BF16), odn, oup, o1d, o2d, o1u, o2u


def solution(mesh):
    fine = Mesh(mesh.devices.reshape(4, 2, 4, 4), ("x", "core", "z", "y"))
    grp, tp = ("x", "core"), ("z", "y")
    rows, slab = P(grp, tp), P(grp, None, tp)
    in_specs = (rows, rows, P(None, tp)) + (slab,) * 6 + (P(grp, None), P(grp, None), P())
    out_specs = (rows, rows) + (slab,) * 6
    return jax.shard_map(local, mesh=fine, in_specs=in_specs, out_specs=out_specs, check_vma=False)
```

```python
import functools

import jax
import jax.numpy as jnp
from jax import lax
from jax.experimental import pallas as pl
from jax.experimental.pallas import tpu as pltpu
from jax.sharding import Mesh, PartitionSpec as P

beta_first = 0.9
beta_second = 0.999
step_rate = 0.2
adam_eps = 1e-08
adapter_scale = 2.0

WIDTH = 8192
RANK = 32
COLS = 512
HALF = 256
ROWS = 512
PROMPTS = 16
ANY = pl.BlockSpec(memory_space=pl.ANY)
VMEM = pl.BlockSpec(memory_space=pltpu.VMEM)
F32 = jnp.float32
BF16 = jnp.bfloat16


def params(mib=60):
    return pltpu.CompilerParams(vmem_limit_bytes=mib * 1024 * 1024)


def pick_kernel(slots, member, down, up, out, pos):
    g = member[0]

    def group(d, carry):
        def step(p, j):
            s = slots[d * PROMPTS + p]
            mine = lax.div(s, PROMPTS) == g

            @pl.when(mine)
            def _():
                i = lax.rem(s, PROMPTS)
                pos[i] = d * 2 + j
                out[d * 2 + j, 0] = down[i]
                out[d * 2 + j, 1] = up[i]

            return j + mine.astype(jnp.int32)

        lax.fori_loop(0, PROMPTS, step, jnp.int32(0), unroll=True)
        return carry

    lax.fori_loop(0, 8, group, 0)


def pick(slots, member, down, up):
    small = jax.ShapeDtypeStruct((PROMPTS,), jnp.int32)
    smem = pl.BlockSpec(memory_space=pltpu.SMEM)
    return pl.pallas_call(
        pick_kernel,
        out_shape=(jax.ShapeDtypeStruct((PROMPTS, 2, RANK, COLS), BF16), small),
        grid_spec=pltpu.PrefetchScalarGridSpec(
            num_scalar_prefetch=2,
            grid=(),
            in_specs=[VMEM, VMEM],
            out_specs=(VMEM, smem),
        ),
        compiler_params=params(),
        cost_estimate=pl.CostEstimate(flops=1, bytes_accessed=1, transcendentals=0),
    )(slots, member, down, up)


def adam_kernel(pos, grads, dn, up, m1d, m2d, m1u, m2u, odn, oup, o1d, o2d, o1u, o2u):
    i0 = pl.program_id(0) * 8
    for k in range(8):
        q = pos[i0 + k]
        for which, (f, m1, m2, of, o1, o2) in enumerate(
            ((dn, m1d, m2d, odn, o1d, o2d), (up, m1u, m2u, oup, o1u, o2u))
        ):
            grad = grads[q, which].astype(F32)
            first = beta_first * m1[k] + (1.0 - beta_first) * grad
            second = beta_second * m2[k] + (1.0 - beta_second) * grad * grad
            of[k] = (
                f[k].astype(F32) - step_rate * first / (jnp.sqrt(second) + adam_eps)
            ).astype(BF16)
            o1[k] = first
            o2[k] = second


def adam(pos, grads, dn, up, m1d, m2d, m1u, m2u):
    block = pl.BlockSpec((8, RANK, COLS), lambda i, pos: (i, 0, 0))
    half = jax.ShapeDtypeStruct((PROMPTS, RANK, COLS), BF16)
    full = jax.ShapeDtypeStruct((PROMPTS, RANK, COLS), F32)
    return pl.pallas_call(
        adam_kernel,
        out_shape=(half, half, full, full, full, full),
        grid_spec=pltpu.PrefetchScalarGridSpec(
            num_scalar_prefetch=1,
            grid=(2,),
            in_specs=[pl.BlockSpec((PROMPTS, 2, RANK, COLS), lambda i, pos: (0, 0, 0, 0))]
            + [block] * 6,
            out_specs=[block] * 6,
        ),
        compiler_params=params(),
        cost_estimate=pl.CostEstimate(flops=1, bytes_accessed=1, transcendentals=0),
    )(pos, grads, dn, up, m1d, m2d, m1u, m2u)


def partial_kernel(where, *refs):
    acts, grads, own, other, weight = refs[0], refs[1:5], refs[5:9], refs[9:13], refs[13]
    forward, backward = refs[14:18], refs[18:22]
    a_held, g_held, w_held, o_held, a_sem, g_sem, w_sem, o_sem = refs[22:]
    x, c, z, y = (where[i] for i in range(4))

    def span(i):
        return pl.ds(i * COLS, COLS)

    a_loads, g_loads, w_loads = [], [], []
    for i in range(4):
        a_loads.append(
            pltpu.make_async_copy(acts.at[lax.rem(y + i, 4)], a_held.at[:, span(i)], a_sem)
        )
        g_loads.append(pltpu.make_async_copy(grads[i], g_held.at[:, span(i)], g_sem))
    for d in range(4):
        for i in range(4):
            if d == 0:
                first = pl.multiple_of((z * 4 + lax.rem(y + i, 4)) * COLS, COLS)
                copies = [(weight.at[pl.ds(first, COLS)], i * COLS, COLS)]
            else:
                turn = lax.rem(x - i + 4, 4) * COLS
                copies = [
                    (own[i].at[d - 1], turn + c * HALF, HALF),
                    (other[i].at[d - 1], turn + (1 - c) * HALF, HALF),
                ]
            for source, first, length in copies:
                rows = pl.ds(pl.multiple_of(first, HALF), length)
                w_loads.append(
                    pltpu.make_async_copy(source, w_held.at[rows, span(d)], w_sem.at[d])
                )
    local, remote = w_loads[:4], w_loads[4:]
    groups = {0: local, 1: remote[:8], 2: remote[8:16], 3: remote[16:]}
    order = (1, 3, 2, 0)
    for copy in a_loads:
        copy.start()
    for d in order:
        for copy in groups[d]:
            copy.start()
    for copy in g_loads:
        copy.start()
    for copy in a_loads:
        copy.wait()
    for d in order:
        for copy in groups[d]:
            copy.wait()
        o_held[d] = jnp.dot(
            a_held[...], w_held[:, span(d)], preferred_element_type=F32
        ).astype(BF16)
        pltpu.make_async_copy(o_held.at[d], forward[d], o_sem.at[d]).start()
    for copy in g_loads:
        copy.wait()
    dims = (((1,), (1,)), ((), ()))
    for i in order:
        o_held[4 + i] = lax.dot_general(
            g_held[...], w_held[span(i)], dims, preferred_element_type=F32
        ).astype(BF16)
        pltpu.make_async_copy(o_held.at[4 + i], backward[i], o_sem.at[4 + i]).start()
    for i in range(4):
        pltpu.make_async_copy(o_held.at[i], forward[i], o_sem.at[i]).wait()
        pltpu.make_async_copy(o_held.at[4 + i], backward[i], o_sem.at[4 + i]).wait()


def partials(where, acts, grads, own, other, weight):
    block = jax.ShapeDtypeStruct((ROWS, COLS), BF16)
    outs = pl.pallas_call(
        partial_kernel,
        out_shape=[block] * 8,
        grid_spec=pltpu.PrefetchScalarGridSpec(
            num_scalar_prefetch=1,
            grid=(),
            in_specs=[ANY] * 14,
            out_specs=[ANY] * 8,
            scratch_shapes=[
                pltpu.VMEM((ROWS, 4 * COLS), BF16),
                pltpu.VMEM((ROWS, 4 * COLS), BF16),
                pltpu.VMEM((4 * COLS, 4 * COLS), BF16),
                pltpu.VMEM((8, ROWS, COLS), BF16),
                pltpu.SemaphoreType.DMA(()),
                pltpu.SemaphoreType.DMA(()),
                pltpu.SemaphoreType.DMA((4,)),
                pltpu.SemaphoreType.DMA((8,)),
            ],
        ),
        compiler_params=params(),
        cost_estimate=pl.CostEstimate(flops=1, bytes_accessed=1, transcendentals=0),
    )(where, acts, *grads, *own, *other, weight)
    return outs[:4], outs[4:]


def grads_kernel(scale_down, scale_up, t0, t1, t2, t3, hot, acts, weighted, out, low_wide, back_wide):
    sums = (t0[...] + t1[...]) + (t2[...] + t3[...])
    low = (scale_down * sums[:RANK]).astype(BF16)
    back = (scale_up * sums[RANK:]).astype(BF16)
    for p in range(PROMPTS):
        rows = pl.ds(p * RANK, RANK)
        low_wide[rows] = hot[p : p + 1, :] * low
        back_wide[rows] = hot[p : p + 1, :] * back
    for which, (scale, wide, other) in enumerate(
        ((scale_down, back_wide, acts), (scale_up, low_wide, weighted))
    ):
        grad = scale * jnp.dot(wide[...], other[...], preferred_element_type=F32)
        out[:, which] = grad.astype(BF16).reshape(PROMPTS, RANK, COLS)


def adapter_grads(terms, hot, acts, weighted, scale_down, scale_up):
    wide = jax.ShapeDtypeStruct((PROMPTS * RANK, ROWS), BF16)
    return pl.pallas_call(
        functools.partial(grads_kernel, scale_down, scale_up),
        out_shape=(jax.ShapeDtypeStruct((PROMPTS, 2, RANK, COLS), BF16), wide, wide),
        in_specs=[VMEM] * 7,
        out_specs=(VMEM,) * 3,
        compiler_params=params(),
        cost_estimate=pl.CostEstimate(flops=1, bytes_accessed=1, transcendentals=0),
    )(*terms, hot, acts, weighted)


def shift(value, axis, by, size=4):
    return lax.ppermute(value, axis, [(i, (i + by) % size) for i in range(size)])


def flip(value, axis, bit, size=4):
    return lax.ppermute(value, axis, [(i, i ^ bit) for i in range(size)])


def local(
    activations,
    output_gradient,
    frozen_weight,
    adapter_down_factors,
    adapter_up_factors,
    first_moment_down,
    second_moment_down,
    first_moment_up,
    second_moment_up,
    sample_row_prompt,
    majority_vote_reward,
    prompt_adapter_slot,
):
    x, c = lax.axis_index("x"), lax.axis_index("core")
    z, y = lax.axis_index("z"), lax.axis_index("y")
    member = x * 2 + c
    scale_down = WIDTH ** (-0.5)
    scale_up = adapter_scale / RANK**0.5

    cuts = [
        [
            lax.dynamic_slice_in_dim(
                frozen_weight,
                lax.rem(z + d, 4) * 2048 + lax.rem(x + y + turn, 4) * COLS + c * HALF,
                HALF,
                axis=0,
            )
            for d in (1, 2, 3)
        ]
        for turn in (0, 2)
    ]
    first = {d: shift(cut, "z", d) for d, cut in zip((1, 2, 3), cuts[0])}
    second = {d: shift(cuts[1][d - 1], "z", d) for d in (1, 3)}
    near = jnp.stack([first[d] for d in (1, 2, 3)])
    cut, _ = lax.optimization_barrier((cuts[1][1], first))
    second[2] = shift(cut, "z", 2)
    far = jnp.stack([second[d] for d in (1, 2, 3)])
    sent, _ = lax.optimization_barrier((near, (second[1], second[3])))
    own = [near, shift(sent, "x", 1), far, shift(sent, "x", 3)]
    swap = [(0, 1), (1, 0)]
    other = {e: lax.ppermute(own[e], "core", swap) for e in (0, 2)}
    slots = prompt_adapter_slot
    slots, _ = lax.optimization_barrier((slots, cuts[0]))
    sent, pos = pick(
        slots, member[None].astype(jnp.int32), adapter_down_factors, adapter_up_factors
    )
    adapters = lax.all_to_all(sent.reshape(8, 2, 2, RANK, COLS), ("x", "core"), 0, 0)
    adapters, _ = lax.optimization_barrier((adapters, (near, second[1], second[3])))
    act, _ = lax.optimization_barrier((activations, adapters))
    acts = lax.all_to_all(jnp.broadcast_to(act[None], (4, ROWS, COLS)), "y", 0, 0)
    down = adapters[:, :, 0].reshape(PROMPTS * RANK, COLS)
    up = adapters[:, :, 1].reshape(PROMPTS * RANK, COLS)

    source = lax.dynamic_slice_in_dim(slots, member * PROMPTS, PROMPTS) // PROMPTS
    ids = jnp.arange(PROMPTS, dtype=jnp.int32)
    before = (source[:, None] == source[None, :]) & (ids[:, None] > ids[None, :])
    order = 2 * source + jnp.sum(before.astype(jnp.int32), axis=1)
    labels = sample_row_prompt[0]
    reward = majority_vote_reward[0].astype(F32)
    label = jnp.sum(jnp.where(labels[None, :] == ids[:, None], order[:, None], 0), axis=0)
    onehot = (label[None, :] == ids[:, None]).astype(F32)
    counts = jnp.sum(onehot, axis=1)
    mean_reward = jnp.sum(onehot * reward[None, :], axis=1) / counts
    advantage = reward - jnp.sum(onehot * mean_reward[:, None], axis=0)
    weighted = (advantage[:, None] * output_gradient.astype(F32)).astype(BF16)

    sent, _ = lax.optimization_barrier((weighted, second[2]))
    grads_in = {0: weighted} | {d: shift(sent, "z", d) for d in (1, 3, 2)}
    late, _ = lax.optimization_barrier(((own[1], own[3]), (grads_in[1], grads_in[3])))
    other[1], other[3] = (lax.ppermute(piece, "core", swap) for piece in late)
    other = [other[e] for e in range(4)]

    contract_cols = (((1,), (1,)), ((), ()))
    low_all = lax.dot_general(down, activations, contract_cols, preferred_element_type=F32)
    back_all = lax.dot_general(up, weighted, contract_cols, preferred_element_type=F32)
    low_part = jnp.sum(low_all.reshape(PROMPTS, RANK, ROWS) * onehot[:, None, :], axis=0)
    back_part = jnp.sum(back_all.reshape(PROMPTS, RANK, ROWS) * onehot[:, None, :], axis=0)
    sums = jnp.concatenate([low_part, back_part])
    sums, _ = lax.optimization_barrier((sums, other))
    sums = sums + sum(shift(sums, "z", i) for i in (1, 3, 2))
    sums, _ = lax.optimization_barrier((sums, (grads_in[1], grads_in[3])))
    terms = [sums] + [shift(sums, "y", i) for i in (1, 3, 2)]
    terms, acts = lax.optimization_barrier((terms, acts))
    where = jnp.stack([x, c, z, y]).astype(jnp.int32)
    layer_parts, input_parts = partials(
        where, acts, [grads_in[i] for i in range(4)], own, other, frozen_weight
    )
    layer_parts = {d: shift(layer_parts[d], "z", -d) if d else layer_parts[d] for d in (1, 3, 2, 0)}
    input_parts = {o: shift(input_parts[o], "y", o) if o else input_parts[o] for o in (1, 3, 2, 0)}
    grads, low_wide, back_wide = adapter_grads(
        terms, onehot.astype(BF16), activations, weighted, scale_down, scale_up
    )
    grads = grads.reshape(8, 2, 2, RANK, COLS)
    grads = lax.all_to_all(grads, ("x", "core"), 0, 0).reshape(PROMPTS, 2, RANK, COLS)
    grads, _ = lax.optimization_barrier((grads, layer_parts[1]))
    updated = adam(
        pos,
        grads,
        adapter_down_factors,
        adapter_up_factors,
        first_moment_down,
        second_moment_down,
        first_moment_up,
        second_moment_up,
    )

    contract_rows = (((0,), (0,)), ((), ()))
    layer = layer_parts[0].astype(F32) + scale_up * lax.dot_general(
        low_wide, up, contract_rows, preferred_element_type=F32
    )
    inward = input_parts[0].astype(F32) + scale_down * lax.dot_general(
        back_wide, down, contract_rows, preferred_element_type=F32
    )
    layer, inward = lax.optimization_barrier((layer, inward))
    for i in (1, 3, 2):
        layer = layer + layer_parts[i].astype(F32)
        inward = inward + input_parts[i].astype(F32)
    odn, oup, o1d, o2d, o1u, o2u = updated
    return layer.astype(BF16), inward.astype(BF16), odn, oup, o1d, o2d, o1u, o2u


def solution(mesh):
    fine = Mesh(mesh.devices.reshape(4, 2, 4, 4), ("x", "core", "z", "y"))
    grp, tp = ("x", "core"), ("z", "y")
    rows, slab = P(grp, tp), P(grp, None, tp)
    in_specs = (rows, rows, P(None, tp)) + (slab,) * 6 + (P(grp, None), P(grp, None), P())
    out_specs = (rows, rows) + (slab,) * 6
    return jax.shard_map(local, mesh=fine, in_specs=in_specs, out_specs=out_specs, check_vma=False)
```

```python
import functools

import jax
import jax.numpy as jnp
from jax import lax
from jax.experimental import pallas as pl
from jax.experimental.pallas import tpu as pltpu
from jax.sharding import Mesh, PartitionSpec as P

beta_first = 0.9
beta_second = 0.999
step_rate = 0.2
adam_eps = 1e-08
adapter_scale = 2.0

WIDTH = 8192
RANK = 32
COLS = 512
HALF = 256
ROWS = 512
PROMPTS = 16
ANY = pl.BlockSpec(memory_space=pl.ANY)
VMEM = pl.BlockSpec(memory_space=pltpu.VMEM)
F32 = jnp.float32
BF16 = jnp.bfloat16


def params(mib=60):
    return pltpu.CompilerParams(vmem_limit_bytes=mib * 1024 * 1024)


def pick_kernel(slots, member, down, up, out, pos):
    g = member[0]

    def group(d, carry):
        def step(p, j):
            s = slots[d * PROMPTS + p]
            mine = lax.div(s, PROMPTS) == g

            @pl.when(mine)
            def _():
                i = lax.rem(s, PROMPTS)
                pos[i] = d * 2 + j
                out[d * 2 + j, 0] = down[i]
                out[d * 2 + j, 1] = up[i]

            return j + mine.astype(jnp.int32)

        lax.fori_loop(0, PROMPTS, step, jnp.int32(0), unroll=True)
        return carry

    lax.fori_loop(0, 8, group, 0)


def pick(slots, member, down, up):
    small = jax.ShapeDtypeStruct((PROMPTS,), jnp.int32)
    smem = pl.BlockSpec(memory_space=pltpu.SMEM)
    return pl.pallas_call(
        pick_kernel,
        out_shape=(jax.ShapeDtypeStruct((PROMPTS, 2, RANK, COLS), BF16), small),
        grid_spec=pltpu.PrefetchScalarGridSpec(
            num_scalar_prefetch=2,
            grid=(),
            in_specs=[VMEM, VMEM],
            out_specs=(VMEM, smem),
        ),
        compiler_params=params(),
        cost_estimate=pl.CostEstimate(flops=1, bytes_accessed=1, transcendentals=0),
    )(slots, member, down, up)


def adam_kernel(pos, grads, dn, up, m1d, m2d, m1u, m2u, odn, oup, o1d, o2d, o1u, o2u):
    i0 = pl.program_id(0) * 8
    for k in range(8):
        q = pos[i0 + k]
        for which, (f, m1, m2, of, o1, o2) in enumerate(
            ((dn, m1d, m2d, odn, o1d, o2d), (up, m1u, m2u, oup, o1u, o2u))
        ):
            grad = grads[q, which].astype(F32)
            first = beta_first * m1[k] + (1.0 - beta_first) * grad
            second = beta_second * m2[k] + (1.0 - beta_second) * grad * grad
            of[k] = (
                f[k].astype(F32) - step_rate * first / (jnp.sqrt(second) + adam_eps)
            ).astype(BF16)
            o1[k] = first
            o2[k] = second


def adam(pos, grads, dn, up, m1d, m2d, m1u, m2u):
    block = pl.BlockSpec((8, RANK, COLS), lambda i, pos: (i, 0, 0))
    half = jax.ShapeDtypeStruct((PROMPTS, RANK, COLS), BF16)
    full = jax.ShapeDtypeStruct((PROMPTS, RANK, COLS), F32)
    return pl.pallas_call(
        adam_kernel,
        out_shape=(half, half, full, full, full, full),
        grid_spec=pltpu.PrefetchScalarGridSpec(
            num_scalar_prefetch=1,
            grid=(2,),
            in_specs=[pl.BlockSpec((PROMPTS, 2, RANK, COLS), lambda i, pos: (0, 0, 0, 0))]
            + [block] * 6,
            out_specs=[block] * 6,
        ),
        compiler_params=params(),
        cost_estimate=pl.CostEstimate(flops=1, bytes_accessed=1, transcendentals=0),
    )(pos, grads, dn, up, m1d, m2d, m1u, m2u)


def partial_kernel(where, *refs):
    acts, grads, own, other, weight = refs[0], refs[1:5], refs[5:9], refs[9:13], refs[13]
    forward, backward = refs[14:18], refs[18:22]
    a_held, g_held, w_held, o_held, a_sem, g_sem, w_sem, o_sem = refs[22:]
    x, c, z, y = (where[i] for i in range(4))

    def span(i):
        return pl.ds(i * COLS, COLS)

    a_loads, g_loads, w_loads = [], [], []
    for i in range(4):
        a_loads.append(
            pltpu.make_async_copy(acts.at[lax.rem(y + i, 4)], a_held.at[:, span(i)], a_sem)
        )
        g_loads.append(pltpu.make_async_copy(grads[i], g_held.at[:, span(i)], g_sem))
    for d in range(4):
        for i in range(4):
            if d == 0:
                first = pl.multiple_of((z * 4 + lax.rem(y + i, 4)) * COLS, COLS)
                copies = [(weight.at[pl.ds(first, COLS)], i * COLS, COLS)]
            else:
                turn = lax.rem(x - i + 4, 4) * COLS
                copies = [
                    (own[i].at[d - 1], turn + c * HALF, HALF),
                    (other[i].at[d - 1], turn + (1 - c) * HALF, HALF),
                ]
            for source, first, length in copies:
                rows = pl.ds(pl.multiple_of(first, HALF), length)
                w_loads.append(
                    pltpu.make_async_copy(source, w_held.at[rows, span(d)], w_sem.at[d])
                )
    local, remote = w_loads[:4], w_loads[4:]
    groups = {0: local, 1: remote[:8], 2: remote[8:16], 3: remote[16:]}
    order = (1, 3, 2, 0)
    for copy in a_loads:
        copy.start()
    for d in order:
        for copy in groups[d]:
            copy.start()
    for copy in g_loads:
        copy.start()
    for copy in a_loads:
        copy.wait()
    for d in order:
        for copy in groups[d]:
            copy.wait()
        o_held[d] = jnp.dot(
            a_held[...], w_held[:, span(d)], preferred_element_type=F32
        ).astype(BF16)
        pltpu.make_async_copy(o_held.at[d], forward[d], o_sem.at[d]).start()
    for copy in g_loads:
        copy.wait()
    dims = (((1,), (1,)), ((), ()))
    for i in order:
        o_held[4 + i] = lax.dot_general(
            g_held[...], w_held[span(i)], dims, preferred_element_type=F32
        ).astype(BF16)
        pltpu.make_async_copy(o_held.at[4 + i], backward[i], o_sem.at[4 + i]).start()
    for i in range(4):
        pltpu.make_async_copy(o_held.at[i], forward[i], o_sem.at[i]).wait()
        pltpu.make_async_copy(o_held.at[4 + i], backward[i], o_sem.at[4 + i]).wait()


def partials(where, acts, grads, own, other, weight):
    block = jax.ShapeDtypeStruct((ROWS, COLS), BF16)
    outs = pl.pallas_call(
        partial_kernel,
        out_shape=[block] * 8,
        grid_spec=pltpu.PrefetchScalarGridSpec(
            num_scalar_prefetch=1,
            grid=(),
            in_specs=[ANY] * 14,
            out_specs=[ANY] * 8,
            scratch_shapes=[
                pltpu.VMEM((ROWS, 4 * COLS), BF16),
                pltpu.VMEM((ROWS, 4 * COLS), BF16),
                pltpu.VMEM((4 * COLS, 4 * COLS), BF16),
                pltpu.VMEM((8, ROWS, COLS), BF16),
                pltpu.SemaphoreType.DMA(()),
                pltpu.SemaphoreType.DMA(()),
                pltpu.SemaphoreType.DMA((4,)),
                pltpu.SemaphoreType.DMA((8,)),
            ],
        ),
        compiler_params=params(),
        cost_estimate=pl.CostEstimate(flops=1, bytes_accessed=1, transcendentals=0),
    )(where, acts, *grads, *own, *other, weight)
    return outs[:4], outs[4:]


def grads_kernel(scale_down, scale_up, t0, t1, t2, t3, hot, acts, weighted, out, low_wide, back_wide):
    sums = (t0[...] + t1[...]) + (t2[...] + t3[...])
    low = (scale_down * sums[:RANK]).astype(BF16)
    back = (scale_up * sums[RANK:]).astype(BF16)
    for p in range(PROMPTS):
        rows = pl.ds(p * RANK, RANK)
        low_wide[rows] = hot[p : p + 1, :] * low
        back_wide[rows] = hot[p : p + 1, :] * back
    for which, (scale, wide, other) in enumerate(
        ((scale_down, back_wide, acts), (scale_up, low_wide, weighted))
    ):
        grad = scale * jnp.dot(wide[...], other[...], preferred_element_type=F32)
        out[:, which] = grad.astype(BF16).reshape(PROMPTS, RANK, COLS)


def adapter_grads(terms, hot, acts, weighted, scale_down, scale_up):
    wide = jax.ShapeDtypeStruct((PROMPTS * RANK, ROWS), BF16)
    return pl.pallas_call(
        functools.partial(grads_kernel, scale_down, scale_up),
        out_shape=(jax.ShapeDtypeStruct((PROMPTS, 2, RANK, COLS), BF16), wide, wide),
        in_specs=[VMEM] * 7,
        out_specs=(VMEM,) * 3,
        compiler_params=params(),
        cost_estimate=pl.CostEstimate(flops=1, bytes_accessed=1, transcendentals=0),
    )(*terms, hot, acts, weighted)


def shift(value, axis, by, size=4):
    return lax.ppermute(value, axis, [(i, (i + by) % size) for i in range(size)])


def flip(value, axis, bit, size=4):
    return lax.ppermute(value, axis, [(i, i ^ bit) for i in range(size)])


def local(
    activations,
    output_gradient,
    frozen_weight,
    adapter_down_factors,
    adapter_up_factors,
    first_moment_down,
    second_moment_down,
    first_moment_up,
    second_moment_up,
    sample_row_prompt,
    majority_vote_reward,
    prompt_adapter_slot,
):
    x, c = lax.axis_index("x"), lax.axis_index("core")
    z, y = lax.axis_index("z"), lax.axis_index("y")
    member = x * 2 + c
    scale_down = WIDTH ** (-0.5)
    scale_up = adapter_scale / RANK**0.5

    cuts = [
        [
            lax.dynamic_slice_in_dim(
                frozen_weight,
                lax.rem(z + d, 4) * 2048 + lax.rem(x + y + turn, 4) * COLS + c * HALF,
                HALF,
                axis=0,
            )
            for d in (1, 2, 3)
        ]
        for turn in (0, 2)
    ]
    first = {d: shift(cut, "z", d) for d, cut in zip((1, 2, 3), cuts[0])}
    second = {d: shift(cuts[1][d - 1], "z", d) for d in (1, 3)}
    near = jnp.stack([first[d] for d in (1, 2, 3)])
    cut, _ = lax.optimization_barrier((cuts[1][1], first))
    second[2] = shift(cut, "z", 2)
    far = jnp.stack([second[d] for d in (1, 2, 3)])
    sent, _ = lax.optimization_barrier((near, (second[1], second[3])))
    own = [near, shift(sent, "x", 1), far, shift(sent, "x", 3)]
    other = [lax.ppermute(piece, "core", [(0, 1), (1, 0)]) for piece in own]
    slots = prompt_adapter_slot
    slots, _ = lax.optimization_barrier((slots, cuts[0]))
    sent, pos = pick(
        slots, member[None].astype(jnp.int32), adapter_down_factors, adapter_up_factors
    )
    adapters = lax.all_to_all(sent.reshape(8, 2, 2, RANK, COLS), ("x", "core"), 0, 0)
    adapters, _ = lax.optimization_barrier((adapters, (near, second[1], second[3])))
    act, _ = lax.optimization_barrier((activations, adapters))
    acts = lax.all_to_all(jnp.broadcast_to(act[None], (4, ROWS, COLS)), "y", 0, 0)
    down = adapters[:, :, 0].reshape(PROMPTS * RANK, COLS)
    up = adapters[:, :, 1].reshape(PROMPTS * RANK, COLS)

    source = lax.dynamic_slice_in_dim(slots, member * PROMPTS, PROMPTS) // PROMPTS
    ids = jnp.arange(PROMPTS, dtype=jnp.int32)
    before = (source[:, None] == source[None, :]) & (ids[:, None] > ids[None, :])
    order = 2 * source + jnp.sum(before.astype(jnp.int32), axis=1)
    labels = sample_row_prompt[0]
    reward = majority_vote_reward[0].astype(F32)
    label = jnp.sum(jnp.where(labels[None, :] == ids[:, None], order[:, None], 0), axis=0)
    onehot = (label[None, :] == ids[:, None]).astype(F32)
    counts = jnp.sum(onehot, axis=1)
    mean_reward = jnp.sum(onehot * reward[None, :], axis=1) / counts
    advantage = reward - jnp.sum(onehot * mean_reward[:, None], axis=0)
    weighted = (advantage[:, None] * output_gradient.astype(F32)).astype(BF16)

    grads_in = {0: weighted}
    sent, _ = lax.optimization_barrier((weighted, second[2]))
    grads_in[1], grads_in[3] = shift(sent, "z", 1), shift(sent, "z", 3)
    sent, _ = lax.optimization_barrier((weighted, (grads_in[1], grads_in[3])))
    grads_in[2] = shift(sent, "z", 2)

    contract_cols = (((1,), (1,)), ((), ()))
    low_all = lax.dot_general(down, activations, contract_cols, preferred_element_type=F32)
    back_all = lax.dot_general(up, weighted, contract_cols, preferred_element_type=F32)
    low_part = jnp.sum(low_all.reshape(PROMPTS, RANK, ROWS) * onehot[:, None, :], axis=0)
    back_part = jnp.sum(back_all.reshape(PROMPTS, RANK, ROWS) * onehot[:, None, :], axis=0)
    sums = jnp.concatenate([low_part, back_part])
    sums, _ = lax.optimization_barrier((sums, other[0]))
    sums = sums + sum(shift(sums, "z", i) for i in (1, 3, 2))
    sums, _ = lax.optimization_barrier((sums, (own[1], own[3], other[0], other[2], grads_in[1], grads_in[3], acts)))
    terms = [sums] + [shift(sums, "y", i) for i in (1, 3, 2)]
    where = jnp.stack([x, c, z, y]).astype(jnp.int32)
    layer_parts, input_parts = partials(
        where, acts, [grads_in[i] for i in range(4)], own, other, frozen_weight
    )
    layer_parts = {d: shift(layer_parts[d], "z", -d) if d else layer_parts[d] for d in (1, 3, 2, 0)}
    input_parts = {o: shift(input_parts[o], "y", o) if o else input_parts[o] for o in (1, 3, 2, 0)}
    grads, low_wide, back_wide = adapter_grads(
        terms, onehot.astype(BF16), activations, weighted, scale_down, scale_up
    )
    grads = grads.reshape(8, 2, 2, RANK, COLS)
    grads = lax.all_to_all(grads, ("x", "core"), 0, 0).reshape(PROMPTS, 2, RANK, COLS)
    grads, _ = lax.optimization_barrier((grads, layer_parts[1]))
    updated = adam(
        pos,
        grads,
        adapter_down_factors,
        adapter_up_factors,
        first_moment_down,
        second_moment_down,
        first_moment_up,
        second_moment_up,
    )

    contract_rows = (((0,), (0,)), ((), ()))
    layer = layer_parts[0].astype(F32) + scale_up * lax.dot_general(
        low_wide, up, contract_rows, preferred_element_type=F32
    )
    inward = input_parts[0].astype(F32) + scale_down * lax.dot_general(
        back_wide, down, contract_rows, preferred_element_type=F32
    )
    inward, updated = lax.optimization_barrier((inward, updated))
    layer = lax.optimization_barrier(layer)
    for i in (1, 3, 2):
        layer = layer + layer_parts[i].astype(F32)
        inward = inward + input_parts[i].astype(F32)
    odn, oup, o1d, o2d, o1u, o2u = updated
    return layer.astype(BF16), inward.astype(BF16), odn, oup, o1d, o2d, o1u, o2u


def solution(mesh):
    fine = Mesh(mesh.devices.reshape(4, 2, 4, 4), ("x", "core", "z", "y"))
    grp, tp = ("x", "core"), ("z", "y")
    rows, slab = P(grp, tp), P(grp, None, tp)
    in_specs = (rows, rows, P(None, tp)) + (slab,) * 6 + (P(grp, None), P(grp, None), P())
    out_specs = (rows, rows) + (slab,) * 6
    return jax.shard_map(local, mesh=fine, in_specs=in_specs, out_specs=out_specs, check_vma=False)
```

```python
import functools

import jax
import jax.numpy as jnp
from jax import lax
from jax.experimental import pallas as pl
from jax.experimental.pallas import tpu as pltpu
from jax.sharding import Mesh, PartitionSpec as P

beta_first = 0.9
beta_second = 0.999
step_rate = 0.2
adam_eps = 1e-08
adapter_scale = 2.0

WIDTH = 8192
RANK = 32
COLS = 512
HALF = 256
ROWS = 512
PROMPTS = 16
ANY = pl.BlockSpec(memory_space=pl.ANY)
VMEM = pl.BlockSpec(memory_space=pltpu.VMEM)
F32 = jnp.float32
BF16 = jnp.bfloat16


def params(mib=60):
    return pltpu.CompilerParams(vmem_limit_bytes=mib * 1024 * 1024)


def pick_kernel(slots, member, down, up, out, pos):
    g = member[0]

    def group(d, carry):
        def step(p, j):
            s = slots[d * PROMPTS + p]
            mine = lax.div(s, PROMPTS) == g

            @pl.when(mine)
            def _():
                i = lax.rem(s, PROMPTS)
                pos[i] = d * 2 + j
                out[d * 2 + j, 0] = down[i]
                out[d * 2 + j, 1] = up[i]

            return j + mine.astype(jnp.int32)

        lax.fori_loop(0, PROMPTS, step, jnp.int32(0))
        return carry

    lax.fori_loop(0, 8, group, 0)


def pick(slots, member, down, up):
    small = jax.ShapeDtypeStruct((PROMPTS,), jnp.int32)
    smem = pl.BlockSpec(memory_space=pltpu.SMEM)
    return pl.pallas_call(
        pick_kernel,
        out_shape=(jax.ShapeDtypeStruct((PROMPTS, 2, RANK, COLS), BF16), small),
        grid_spec=pltpu.PrefetchScalarGridSpec(
            num_scalar_prefetch=2,
            grid=(),
            in_specs=[VMEM, VMEM],
            out_specs=(VMEM, smem),
        ),
        compiler_params=params(),
        cost_estimate=pl.CostEstimate(flops=1, bytes_accessed=1, transcendentals=0),
    )(slots, member, down, up)


def adam_kernel(pos, grads, dn, up, m1d, m2d, m1u, m2u, odn, oup, o1d, o2d, o1u, o2u):
    i0 = pl.program_id(0) * 8
    for k in range(8):
        q = pos[i0 + k]
        for which, (f, m1, m2, of, o1, o2) in enumerate(
            ((dn, m1d, m2d, odn, o1d, o2d), (up, m1u, m2u, oup, o1u, o2u))
        ):
            grad = grads[q, which].astype(F32)
            first = beta_first * m1[k] + (1.0 - beta_first) * grad
            second = beta_second * m2[k] + (1.0 - beta_second) * grad * grad
            of[k] = (
                f[k].astype(F32) - step_rate * first / (jnp.sqrt(second) + adam_eps)
            ).astype(BF16)
            o1[k] = first
            o2[k] = second


def adam(pos, grads, dn, up, m1d, m2d, m1u, m2u):
    block = pl.BlockSpec((8, RANK, COLS), lambda i, pos: (i, 0, 0))
    half = jax.ShapeDtypeStruct((PROMPTS, RANK, COLS), BF16)
    full = jax.ShapeDtypeStruct((PROMPTS, RANK, COLS), F32)
    return pl.pallas_call(
        adam_kernel,
        out_shape=(half, half, full, full, full, full),
        grid_spec=pltpu.PrefetchScalarGridSpec(
            num_scalar_prefetch=1,
            grid=(2,),
            in_specs=[pl.BlockSpec((PROMPTS, 2, RANK, COLS), lambda i, pos: (0, 0, 0, 0))]
            + [block] * 6,
            out_specs=[block] * 6,
        ),
        compiler_params=params(),
        cost_estimate=pl.CostEstimate(flops=1, bytes_accessed=1, transcendentals=0),
    )(pos, grads, dn, up, m1d, m2d, m1u, m2u)


def partial_kernel(where, *refs):
    acts, grads, own, other, weight = refs[0], refs[1:5], refs[5:9], refs[9:13], refs[13]
    forward, backward = refs[14:18], refs[18:22]
    a_held, g_held, w_held, o_held, a_sem, g_sem, w_sem, o_sem = refs[22:]
    x, c, z, y = (where[i] for i in range(4))

    def span(i):
        return pl.ds(i * COLS, COLS)

    a_loads, g_loads, w_loads = [], [], []
    for i in range(4):
        a_loads.append(
            pltpu.make_async_copy(acts.at[lax.rem(y + i, 4)], a_held.at[:, span(i)], a_sem)
        )
        g_loads.append(pltpu.make_async_copy(grads[i], g_held.at[:, span(i)], g_sem))
    for d in range(4):
        for i in range(4):
            if d == 0:
                first = pl.multiple_of((z * 4 + lax.rem(y + i, 4)) * COLS, COLS)
                copies = [(weight.at[pl.ds(first, COLS)], i * COLS, COLS)]
            else:
                turn = lax.rem(x - i + 4, 4) * COLS
                copies = [
                    (own[i].at[d - 1], turn + c * HALF, HALF),
                    (other[i].at[d - 1], turn + (1 - c) * HALF, HALF),
                ]
            for source, first, length in copies:
                rows = pl.ds(pl.multiple_of(first, HALF), length)
                w_loads.append(
                    pltpu.make_async_copy(source, w_held.at[rows, span(d)], w_sem.at[d])
                )
    local, remote = w_loads[:4], w_loads[4:]
    groups = {0: local, 1: remote[:8], 2: remote[8:16], 3: remote[16:]}
    order = (1, 3, 2, 0)
    for copy in a_loads:
        copy.start()
    for d in order:
        for copy in groups[d]:
            copy.start()
    for copy in g_loads:
        copy.start()
    for copy in a_loads:
        copy.wait()
    for d in order:
        for copy in groups[d]:
            copy.wait()
        o_held[d] = jnp.dot(
            a_held[...], w_held[:, span(d)], preferred_element_type=F32
        ).astype(BF16)
        pltpu.make_async_copy(o_held.at[d], forward[d], o_sem.at[d]).start()
    for copy in g_loads:
        copy.wait()
    dims = (((1,), (1,)), ((), ()))
    for i in order:
        o_held[4 + i] = lax.dot_general(
            g_held[...], w_held[span(i)], dims, preferred_element_type=F32
        ).astype(BF16)
        pltpu.make_async_copy(o_held.at[4 + i], backward[i], o_sem.at[4 + i]).start()
    for i in range(4):
        pltpu.make_async_copy(o_held.at[i], forward[i], o_sem.at[i]).wait()
        pltpu.make_async_copy(o_held.at[4 + i], backward[i], o_sem.at[4 + i]).wait()


def partials(where, acts, grads, own, other, weight):
    block = jax.ShapeDtypeStruct((ROWS, COLS), BF16)
    outs = pl.pallas_call(
        partial_kernel,
        out_shape=[block] * 8,
        grid_spec=pltpu.PrefetchScalarGridSpec(
            num_scalar_prefetch=1,
            grid=(),
            in_specs=[ANY] * 14,
            out_specs=[ANY] * 8,
            scratch_shapes=[
                pltpu.VMEM((ROWS, 4 * COLS), BF16),
                pltpu.VMEM((ROWS, 4 * COLS), BF16),
                pltpu.VMEM((4 * COLS, 4 * COLS), BF16),
                pltpu.VMEM((8, ROWS, COLS), BF16),
                pltpu.SemaphoreType.DMA(()),
                pltpu.SemaphoreType.DMA(()),
                pltpu.SemaphoreType.DMA((4,)),
                pltpu.SemaphoreType.DMA((8,)),
            ],
        ),
        compiler_params=params(),
        cost_estimate=pl.CostEstimate(flops=1, bytes_accessed=1, transcendentals=0),
    )(where, acts, *grads, *own, *other, weight)
    return outs[:4], outs[4:]


def shift(value, axis, by, size=4):
    return lax.ppermute(value, axis, [(i, (i + by) % size) for i in range(size)])


def flip(value, axis, bit, size=4):
    return lax.ppermute(value, axis, [(i, i ^ bit) for i in range(size)])


def local(
    activations,
    output_gradient,
    frozen_weight,
    adapter_down_factors,
    adapter_up_factors,
    first_moment_down,
    second_moment_down,
    first_moment_up,
    second_moment_up,
    sample_row_prompt,
    majority_vote_reward,
    prompt_adapter_slot,
):
    x, c = lax.axis_index("x"), lax.axis_index("core")
    z, y = lax.axis_index("z"), lax.axis_index("y")
    member = x * 2 + c
    scale_down = WIDTH ** (-0.5)
    scale_up = adapter_scale / RANK**0.5

    cuts = [
        [
            lax.dynamic_slice_in_dim(
                frozen_weight,
                lax.rem(z + d, 4) * 2048 + lax.rem(x + y + turn, 4) * COLS + c * HALF,
                HALF,
                axis=0,
            )
            for d in (1, 2, 3)
        ]
        for turn in (0, 2)
    ]
    first = {d: shift(cut, "z", d) for d, cut in zip((1, 2, 3), cuts[0])}
    second = {d: shift(cuts[1][d - 1], "z", d) for d in (1, 3)}
    near = jnp.stack([first[d] for d in (1, 2, 3)])
    cut, _ = lax.optimization_barrier((cuts[1][1], first))
    second[2] = shift(cut, "z", 2)
    far = jnp.stack([second[d] for d in (1, 2, 3)])
    sent, _ = lax.optimization_barrier((near, (second[1], second[3])))
    own = [near, shift(sent, "x", 1), far, shift(sent, "x", 3)]
    other = [lax.ppermute(piece, "core", [(0, 1), (1, 0)]) for piece in own]
    slots = prompt_adapter_slot
    slots, _ = lax.optimization_barrier((slots, cuts[0]))
    sent, pos = pick(
        slots, member[None].astype(jnp.int32), adapter_down_factors, adapter_up_factors
    )
    adapters = lax.all_to_all(sent.reshape(8, 2, 2, RANK, COLS), ("x", "core"), 0, 0)
    adapters, _ = lax.optimization_barrier((adapters, (near, second[1], second[3])))
    act, _ = lax.optimization_barrier((activations, adapters))
    acts = lax.all_to_all(jnp.broadcast_to(act[None], (4, ROWS, COLS)), "y", 0, 0)
    down = adapters[:, :, 0].reshape(PROMPTS * RANK, COLS)
    up = adapters[:, :, 1].reshape(PROMPTS * RANK, COLS)

    source = lax.dynamic_slice_in_dim(slots, member * PROMPTS, PROMPTS) // PROMPTS
    ids = jnp.arange(PROMPTS, dtype=jnp.int32)
    before = (source[:, None] == source[None, :]) & (ids[:, None] > ids[None, :])
    order = 2 * source + jnp.sum(before.astype(jnp.int32), axis=1)
    labels = sample_row_prompt[0]
    reward = majority_vote_reward[0].astype(F32)
    label = jnp.sum(jnp.where(labels[None, :] == ids[:, None], order[:, None], 0), axis=0)
    onehot = (label[None, :] == ids[:, None]).astype(F32)
    counts = jnp.sum(onehot, axis=1)
    mean_reward = jnp.sum(onehot * reward[None, :], axis=1) / counts
    advantage = reward - jnp.sum(onehot * mean_reward[:, None], axis=0)
    weighted = (advantage[:, None] * output_gradient.astype(F32)).astype(BF16)

    grads_in = {0: weighted}
    sent, _ = lax.optimization_barrier((weighted, second[2]))
    grads_in[1], grads_in[3] = shift(sent, "z", 1), shift(sent, "z", 3)
    sent, _ = lax.optimization_barrier((weighted, (grads_in[1], grads_in[3])))
    grads_in[2] = shift(sent, "z", 2)

    contract_cols = (((1,), (1,)), ((), ()))
    low_all = lax.dot_general(down, activations, contract_cols, preferred_element_type=F32)
    back_all = lax.dot_general(up, weighted, contract_cols, preferred_element_type=F32)
    low_part = jnp.sum(low_all.reshape(PROMPTS, RANK, ROWS) * onehot[:, None, :], axis=0)
    back_part = jnp.sum(back_all.reshape(PROMPTS, RANK, ROWS) * onehot[:, None, :], axis=0)
    sums = jnp.concatenate([low_part, back_part])
    sums = sums + sum(shift(sums, "z", i) for i in (1, 3, 2))
    sums, _ = lax.optimization_barrier((sums, (own[1], own[3], other[0], other[2], grads_in[1], grads_in[3], acts)))
    sums = sums + sum(shift(sums, "y", i) for i in (1, 3, 2))
    low = (scale_down * sums[:RANK]).astype(BF16)
    back_low = (scale_up * sums[RANK:]).astype(BF16)
    half = onehot.astype(BF16)
    low_wide = (half[:, None, :] * low[None, :, :]).reshape(PROMPTS * RANK, ROWS)
    back_wide = (half[:, None, :] * back_low[None, :, :]).reshape(PROMPTS * RANK, ROWS)
    where = jnp.stack([x, c, z, y]).astype(jnp.int32)
    layer_parts, input_parts = partials(
        where, acts, [grads_in[i] for i in range(4)], own, other, frozen_weight
    )
    layer_parts = {d: shift(layer_parts[d], "z", -d) if d else layer_parts[d] for d in (1, 3, 2, 0)}
    input_parts = {o: shift(input_parts[o], "y", o) if o else input_parts[o] for o in (1, 3, 2, 0)}
    grad_down = scale_down * jnp.dot(back_wide, activations, preferred_element_type=F32)
    grad_up = scale_up * jnp.dot(low_wide, weighted, preferred_element_type=F32)
    grads = jnp.stack(
        [
            grad_down.astype(BF16).reshape(8, 2, RANK, COLS),
            grad_up.astype(BF16).reshape(8, 2, RANK, COLS),
        ],
        axis=2,
    )
    grads = lax.all_to_all(grads, ("x", "core"), 0, 0).reshape(PROMPTS, 2, RANK, COLS)
    grads, _ = lax.optimization_barrier((grads, layer_parts[1]))
    updated = adam(
        pos,
        grads,
        adapter_down_factors,
        adapter_up_factors,
        first_moment_down,
        second_moment_down,
        first_moment_up,
        second_moment_up,
    )

    contract_rows = (((0,), (0,)), ((), ()))
    layer = layer_parts[0].astype(F32) + scale_up * lax.dot_general(
        low_wide, up, contract_rows, preferred_element_type=F32
    )
    inward = input_parts[0].astype(F32) + scale_down * lax.dot_general(
        back_wide, down, contract_rows, preferred_element_type=F32
    )
    inward, updated = lax.optimization_barrier((inward, updated))
    layer = lax.optimization_barrier(layer)
    for i in (1, 3, 2):
        layer = layer + layer_parts[i].astype(F32)
        inward = inward + input_parts[i].astype(F32)
    odn, oup, o1d, o2d, o1u, o2u = updated
    return layer.astype(BF16), inward.astype(BF16), odn, oup, o1d, o2d, o1u, o2u


def solution(mesh):
    fine = Mesh(mesh.devices.reshape(4, 2, 4, 4), ("x", "core", "z", "y"))
    grp, tp = ("x", "core"), ("z", "y")
    rows, slab = P(grp, tp), P(grp, None, tp)
    in_specs = (rows, rows, P(None, tp)) + (slab,) * 6 + (P(grp, None), P(grp, None), P())
    out_specs = (rows, rows) + (slab,) * 6
    return jax.shard_map(local, mesh=fine, in_specs=in_specs, out_specs=out_specs, check_vma=False)
```
